32 devices in a mesh: grp: 2 (over x), lat: 16 (over z, y, core).
Axes of the slice: x: 2, y: 2, z: 4, core: 2. Of those that a mesh axis runs over, the one named last changes fastest.
Arguments:
- gauge: float32 [4, 2, 3, 3, 16, 4, 256], P(None, None, None, None, 'lat', 'grp'), may hold values from -2.5 to 2.5
- amplitudes: float32 [2, 2, 3, 16, 32], P(None, None, None, 'lat'), may hold values from -600 to 600
- source_sites: int32 [2, 16, 32], P(None, 'lat'), may hold values from 0 to 1023
- spin_weights: float32 [2, 2, 4], replicated, may hold values from -4 to 4
Outputs:
- propagator: float32 [2, 2, 4, 3, 16, 4, 256], P(None, None, None, None, 'lat', 'grp')
The draws below stay inside these ranges and needn't reach their ends.
Inputs may be any that keep to these rules, and one draw needn't show every extreme that they name: source_sites[r, t, p] is the spatial site z * 16 * 16 + y * 16 + x of point p of side r on time slice t; points may coincide.
All inputs are finite; a program needn't handle non-finite values.
Results may differ from the reference program's by a relative error of at most 0.0001.
Values sent between devices are 32-bit elements; how exact they have to be, the bound alone decides.
A program may use at most 64 MiB of HBM per device.

```python
import jax
import jax.numpy as jnp
from jax import lax

LXY = 16
NPTS = 32
N_SMEAR = 4
ITERS = 4
RHS = 2
NZ = 4
NT = 16


def touch_ends(drawn, key, smallest, top_value):
    longest = drawn.shape.index(max(drawn.shape))
    spots = []
    for shift in (0, 1):
        where = [jax.random.randint(jax.random.fold_in(key, axis), (), 0, length) for axis, length in enumerate(drawn.shape)]
        where[longest] = (where[longest] + shift) % drawn.shape[longest]
        spots.append(tuple(where))
    return drawn.at[spots[0]].set(smallest).at[spots[1]].set(top_value)


def block_levels(stream_key, extent, split, smallest, high):
    def one(dim, shards_of):
        steps = jax.random.uniform(jax.random.fold_in(jax.random.fold_in(stream_key, 6), dim), (shards_of,), jnp.float32, smallest / len(split), high / len(split))
        return jnp.repeat(jnp.exp(steps), extent[dim] // shards_of).reshape((-1,) + (1,) * (len(extent) - dim - 1))

    loudness = one(*split[0])
    for cut in split[1:]:
        loudness = loudness * one(*cut)
    return loudness


def gaussian(own_key, dims, deviation, limit, shards=(), kind=jnp.bfloat16):
    entries = deviation * jax.random.normal(own_key, dims, jnp.float32)
    if shards:
        entries = entries * block_levels(own_key, dims, shards, -0.22, 0.18)
    return jnp.clip(entries, -limit, limit).astype(kind)


def setup_inputs(seed: int = 0) -> dict:
    splits = jax.random.split(jax.random.key(seed), 5)
    gauge = gaussian(splits[0], (4, 2, 3, 3, NT, NZ, LXY * LXY), 6 ** -0.5, 2.5, ((4, 16), (5, 2)), jnp.float32)
    amplitudes = gaussian(splits[1], (RHS, 2, 3, NT, NPTS), 100.0, 600.0, ((3, 16),), jnp.float32)
    source_sites = touch_ends(jax.random.randint(splits[2], (RHS, NT, NPTS), 0, NZ * LXY * LXY), jax.random.fold_in(splits[2], 1), 0, (NZ * LXY * LXY) - 1).astype(jnp.int32)
    spin_weights = gaussian(splits[3], (RHS, 2, 4), 1.0, 4.0, (), jnp.float32)
    return {"gauge": gauge, "amplitudes": amplitudes, "source_sites": source_sites, "spin_weights": spin_weights}


smear_weight = 0.2
hop_kappa = 0.125
gamma_perm = ((3, 2, 1, 0), (3, 2, 1, 0), (2, 3, 0, 1), (2, 3, 0, 1))
gamma_phase = ((1, 1, 3, 3), (2, 0, 0, 2), (1, 3, 3, 1), (0, 0, 0, 0))


def phase_times(code, real, imag):
    if code == 0:
        return real, imag
    if code == 1:
        return -imag, real
    if code == 2:
        return -real, -imag
    return imag, -real


def apply_gamma(hop_dir, field):
    rows_re = []
    rows_im = []
    for spin in range(4):
        picked = field[:, :, gamma_perm[hop_dir][spin]]
        real, imag = phase_times(gamma_phase[hop_dir][spin], picked[:, 0], picked[:, 1])
        rows_re.append(real)
        rows_im.append(imag)
    return jnp.stack([jnp.stack(rows_re, 1), jnp.stack(rows_im, 1)], 1)


def colour_times(links, field):
    link_re = links[0][None, None]
    link_im = links[1][None, None]
    field_re = field[:, 0][:, :, None]
    field_im = field[:, 1][:, :, None]
    out_re = jnp.sum(link_re * field_re - link_im * field_im, axis=3)
    out_im = jnp.sum(link_re * field_im + link_im * field_re, axis=3)
    return jnp.stack([out_re, out_im], 1)


def adjoint(links):
    return jnp.stack([jnp.swapaxes(links[0], 0, 1), -jnp.swapaxes(links[1], 0, 1)])


def roll_site(field, hop_dir, offset):
    if hop_dir == 2:
        return jnp.roll(field, offset, axis=-2)
    shape = field.shape
    grid = field.reshape(shape[:-1] + (LXY, LXY))
    grid = jnp.roll(grid, offset, axis=-1 - hop_dir)
    return grid.reshape(shape)


def time_next(field):
    return jnp.concatenate([field[..., 1:, :, :], -field[..., :1, :, :]], axis=-3)


def time_prev(field):
    return jnp.concatenate([-field[..., -1:, :, :], field[..., :-1, :, :]], axis=-3)


def smear_step(colour_field, gauge):
    total = colour_field
    for hop_dir in range(3):
        total = total + smear_weight * colour_times(gauge[hop_dir], roll_site(colour_field, hop_dir, -1))
        total = total + smear_weight * roll_site(colour_times(adjoint(gauge[hop_dir]), colour_field), hop_dir, 1)
    return total / (1.0 + 6.0 * smear_weight)


def hopping(spinor, gauge):
    total = jnp.zeros_like(spinor)
    for hop_dir in range(4):
        if hop_dir < 3:
            ahead = roll_site(spinor, hop_dir, -1)
        else:
            ahead = time_next(spinor)
        forward = colour_times(gauge[hop_dir], ahead)
        total = total + forward - apply_gamma(hop_dir, forward)
        back = colour_times(adjoint(gauge[hop_dir]), spinor)
        if hop_dir < 3:
            back = roll_site(back, hop_dir, 1)
        else:
            back = time_prev(back)
        total = total + back + apply_gamma(hop_dir, back)
    return total


def spin_expand(colour_field, weights):
    weight_re = weights[:, 0][:, :, None, None, None, None]
    weight_im = weights[:, 1][:, :, None, None, None, None]
    field_re = colour_field[:, 0]
    field_im = colour_field[:, 1]
    out_re = weight_re * field_re - weight_im * field_im
    out_im = weight_re * field_im + weight_im * field_re
    return jnp.stack([out_re, out_im], 1)


def reference(gauge, amplitudes, source_sites, spin_weights):
    count = NZ * LXY * LXY
    row_index = jnp.broadcast_to(jnp.arange(RHS, dtype=jnp.int32)[:, None, None], source_sites.shape)
    time_index = jnp.broadcast_to(jnp.arange(NT, dtype=jnp.int32)[None, :, None], source_sites.shape)
    values = jnp.transpose(amplitudes, (0, 3, 4, 1, 2))
    flat = jnp.zeros((RHS, NT, count, 2, 3), amplitudes.dtype)
    flat = flat.at[row_index, time_index, source_sites].add(values)
    colour_all = jnp.transpose(flat, (0, 3, 4, 1, 2)).reshape((RHS, 2, 1, 3, NT, NZ, LXY * LXY))

    def one_side(items):
        colour_field, weights = items
        colour_field = colour_field[None]
        for smear_index in range(N_SMEAR):
            colour_field = smear_step(colour_field, gauge)
        source = spin_expand(colour_field, weights[None])
        spinor = source
        for iteration in range(ITERS):
            spinor = source + hop_kappa * hopping(spinor, gauge)
        return spinor[0]

    return lax.map(one_side, (colour_all, spin_weights))
```

```python
import functools

import jax
import jax.numpy as jnp
from jax import lax
from jax.experimental import pallas as pl
from jax.experimental.pallas import tpu as pltpu
from jax.sharding import PartitionSpec as P

LXY = 16
LANES = 128
N_SMEAR = 4
ITERS = 4

smear_weight = 0.2
hop_kappa = 0.125
gamma_perm = ((3, 2, 1, 0), (3, 2, 1, 0), (2, 3, 0, 1), (2, 3, 0, 1))
gamma_phase = ((1, 1, 3, 3), (2, 0, 0, 2), (1, 3, 3, 1), (0, 0, 0, 0))


def phase_times(code, real, imag):
    if code == 0:
        return (real, imag)
    if code == 1:
        return (-imag, real)
    if code == 2:
        return (-real, -imag)
    return (imag, -real)


def project(hop_dir, sign, psi):
    re, im = psi
    rows_re, rows_im = [], []
    for spin in range(2):
        other = gamma_perm[hop_dir][spin]
        p_re, p_im = phase_times(gamma_phase[hop_dir][spin], re[other], im[other])
        if sign > 0:
            rows_re.append(re[spin] + p_re)
            rows_im.append(im[spin] + p_im)
        else:
            rows_re.append(re[spin] - p_re)
            rows_im.append(im[spin] - p_im)
    return jnp.stack(rows_re), jnp.stack(rows_im)


def add_rows(hop_dir, sign, total, half):
    t_re, t_im = list(total[0]), list(total[1])
    h_re, h_im = half
    for spin in range(2):
        t_re[spin] = t_re[spin] + h_re[spin]
        t_im[spin] = t_im[spin] + h_im[spin]
    for spin in (2, 3):
        other = gamma_perm[hop_dir][spin]
        p_re, p_im = phase_times(gamma_phase[hop_dir][spin], h_re[other], h_im[other])
        if sign > 0:
            t_re[spin] = t_re[spin] + p_re
            t_im[spin] = t_im[spin] + p_im
        else:
            t_re[spin] = t_re[spin] - p_re
            t_im[spin] = t_im[spin] - p_im
    return t_re, t_im


def times_link(links, half, adjoint):
    h_re, h_im = half
    out_re = out_im = None
    for b in range(3):
        if adjoint:
            u_re = links[0, b][None]
            u_im = -links[1, b][None]
        else:
            u_re = jnp.stack([links[0, a, b] for a in range(3)])[None]
            u_im = jnp.stack([links[1, a, b] for a in range(3)])[None]
        b_re = h_re[:, b][:, None]
        b_im = h_im[:, b][:, None]
        t_re = u_re * b_re - u_im * b_im
        t_im = u_re * b_im + u_im * b_re
        out_re = t_re if out_re is None else out_re + t_re
        out_im = t_im if out_im is None else out_im + t_im
    return out_re, out_im


def kernel(
    groups, sheets, thick, amp_ref, site_ref, weight_ref, gauge_ref, out_ref,
    recv, links, send_t, recv_t, stage, src,
    own_sem, g_send, g_recv, t_send, t_recv, f_send, f_recv,
):
    nz = groups * thick
    rows = 2 * nz
    group = lax.axis_index("grp")
    sheet = lax.axis_index("lat")
    ahead = lax.rem(sheet + 1, sheets)
    behind = lax.rem(sheet + sheets - 1, sheets)
    parts = ((0, 54), (54, 18))

    own = [
        pltpu.make_async_copy(
            gauge_ref.at[pl.ds(lo, n)], recv.at[group, pl.ds(lo, n)], own_sem.at[i]
        )
        for i, (lo, n) in enumerate(parts)
    ]
    for copy in own:
        copy.start()

    barrier = pltpu.get_barrier_semaphore()
    for k in range(1, groups):
        pl.semaphore_signal(barrier, inc=1, device_id={"grp": lax.rem(group + k, groups)})
    pl.semaphore_signal(barrier, inc=1, device_id={"lat": ahead})
    pl.semaphore_signal(barrier, inc=1, device_id={"lat": behind})
    pl.semaphore_wait(barrier, groups + 1)

    def gauge_copy(part, k, slot):
        lo, n = parts[part]
        return pltpu.make_async_remote_copy(
            src_ref=gauge_ref.at[pl.ds(lo, n)],
            dst_ref=recv.at[slot, pl.ds(lo, n)],
            send_sem=g_send.at[part, k],
            recv_sem=g_recv.at[part, k],
            device_id={"grp": lax.rem(group + k, groups)},
        )

    for part in range(2):
        for k in range(1, groups):
            gauge_copy(part, k, group).start()

    row = lax.broadcasted_iota(jnp.int32, (rows, LANES), 0)
    lane = lax.broadcasted_iota(jnp.int32, (rows, LANES), 1)
    upper_half = row >= nz
    z = jnp.where(upper_half, row - nz, row)
    col = lane % LXY

    def shifted(field, hop_dir, offset):
        lanes_axis, rows_axis = field.ndim - 1, field.ndim - 2
        if hop_dir == 0:
            if offset > 0:
                return jnp.where(
                    col == LXY - 1,
                    pltpu.roll(field, LXY - 1, lanes_axis),
                    pltpu.roll(field, LANES - 1, lanes_axis),
                )
            return jnp.where(
                col == 0,
                pltpu.roll(field, LANES - LXY + 1, lanes_axis),
                pltpu.roll(field, 1, lanes_axis),
            )
        if hop_dir == 1:
            if offset > 0:
                rolled = pltpu.roll(field, LANES - LXY, lanes_axis)
                edge = lane >= LANES - LXY
            else:
                rolled = pltpu.roll(field, LXY, lanes_axis)
                edge = lane < LXY
            return jnp.where(edge, pltpu.roll(rolled, nz, rows_axis), rolled)
        if offset > 0:
            return jnp.where(
                z == nz - 1,
                pltpu.roll(field, nz - 1, rows_axis),
                pltpu.roll(field, rows - 1, rows_axis),
            )
        return jnp.where(
            z == 0,
            pltpu.roll(field, rows - nz + 1, rows_axis),
            pltpu.roll(field, 1, rows_axis),
        )

    def shifted_pair(pair, hop_dir, offset):
        return shifted(pair[0], hop_dir, offset), shifted(pair[1], hop_dir, offset)

    cells = z * (2 * LANES) + jnp.where(upper_half, LANES, 0) + lane
    points = site_ref.shape[2]

    def add_point(p, fields):
        hit = cells == site_ref[group, 0, p]
        return tuple(
            fields[i] + jnp.where(hit, amp_ref[group, i // 3, i % 3, 0, p], 0.0)
            for i in range(6)
        )

    zero = jnp.zeros((rows, LANES), jnp.float32)
    fields = lax.fori_loop(0, points, add_point, (zero,) * 6)
    colour = (jnp.stack(fields[:3])[None], jnp.stack(fields[3:])[None])

    def arrange(part):
        lo, n = parts[part]
        own[part].wait()
        for k in range(1, groups):
            gauge_copy(part, k, lax.rem(group + groups - k, groups)).wait_recv()
        for owner in range(groups):
            for half in range(2):
                to = half * nz + owner * thick
                links[pl.ds(lo, n), to : to + thick, :] = recv[
                    owner, pl.ds(lo, n), half * thick : (half + 1) * thick, :
                ]

    def link(hop_dir):
        class View:
            def __getitem__(self, index):
                base = hop_dir * 18 + index[0] * 9 + index[1] * 3
                if len(index) == 3:
                    return links[base + index[2]]
                return links[base : base + 3]

        return View()

    arrange(0)
    norm = 1.0 + 6.0 * smear_weight

    def smear(_, colour):
        total = None
        for hop_dir in range(3):
            fwd = times_link(link(hop_dir), shifted_pair(colour, hop_dir, 1), False)
            back = shifted_pair(times_link(link(hop_dir), colour, True), hop_dir, -1)
            add = (fwd[0] + back[0], fwd[1] + back[1])
            total = add if total is None else (total[0] + add[0], total[1] + add[1])
        return tuple(
            (1.0 / norm) * colour[i] + (smear_weight / norm) * total[i] for i in range(2)
        )

    colour = lax.fori_loop(0, N_SMEAR, smear, colour)
    c_re, c_im = colour[0][0], colour[1][0]
    for spin in range(4):
        w_re = weight_ref[group, 0, spin]
        w_im = weight_ref[group, 1, spin]
        src[0, spin] = w_re * c_re - w_im * c_im
        src[1, spin] = w_re * c_im + w_im * c_re

    arrange(1)
    sign_low = jnp.where(sheet == 0, -1.0, 1.0).astype(jnp.float32)
    sign_high = jnp.where(sheet == sheets - 1, -1.0, 1.0).astype(jnp.float32)

    def t_copy(step, way):
        return pltpu.make_async_remote_copy(
            src_ref=send_t.at[step, way],
            dst_ref=recv_t.at[step, way],
            send_sem=t_send.at[step, way],
            recv_sem=t_recv.at[step, way],
            device_id={"lat": behind if way == 0 else ahead},
        )

    def hop(step, psi):
        psi = (psi[0], psi[1])
        minus = project(3, -1, psi)
        send_t[step, 0, 0] = minus[0]
        send_t[step, 0, 1] = minus[1]
        t_copy(step, 0).start()
        plus = times_link(link(3), project(3, 1, psi), True)
        send_t[step, 1, 0] = plus[0]
        send_t[step, 1, 1] = plus[1]
        t_copy(step, 1).start()
        zeros = jnp.zeros((3, rows, LANES), jnp.float32)
        total = ([zeros] * 4, [zeros] * 4)
        for hop_dir in range(3):
            half = shifted_pair(project(hop_dir, -1, psi), hop_dir, 1)
            total = add_rows(hop_dir, -1, total, times_link(link(hop_dir), half, False))
            half = times_link(link(hop_dir), project(hop_dir, 1, psi), True)
            total = add_rows(hop_dir, 1, total, shifted_pair(half, hop_dir, -1))
        t_copy(step, 0).wait_recv()
        half = (sign_high * recv_t[step, 0, 0], sign_high * recv_t[step, 0, 1])
        total = add_rows(3, -1, total, times_link(link(3), half, False))
        t_copy(step, 1).wait_recv()
        half = (sign_low * recv_t[step, 1, 0], sign_low * recv_t[step, 1, 1])
        total = add_rows(3, 1, total, half)
        return tuple(src[i] + hop_kappa * jnp.stack(total[i]) for i in range(2))

    psi = lax.fori_loop(0, ITERS, hop, (src[0], src[1]))

    for owner in range(groups):
        for half in range(2):
            at = half * nz + owner * thick
            for i in range(2):
                stage[owner, i, :, :, half * thick : (half + 1) * thick, :] = psi[i][
                    :, :, at : at + thick, :
                ]

    def final_copy(k, slot, to):
        return pltpu.make_async_remote_copy(
            src_ref=stage.at[slot],
            dst_ref=out_ref.at[to],
            send_sem=f_send.at[k],
            recv_sem=f_recv.at[k],
            device_id={"grp": lax.rem(group + k, groups)},
        )

    for k in range(1, groups):
        final_copy(k, lax.rem(group + k, groups), group).start()
    mine = pltpu.make_async_copy(stage.at[group], out_ref.at[group], own_sem.at[2])
    mine.start()

    for part in range(2):
        for k in range(1, groups):
            gauge_copy(part, k, group).wait_send()
    for step in range(ITERS):
        for way in range(2):
            t_copy(step, way).wait_send()
    mine.wait()
    for k in range(1, groups):
        final_copy(k, lax.rem(group + k, groups), group).wait_send()
        final_copy(k, group, lax.rem(group + groups - k, groups)).wait_recv()


def on_device(gauge, amplitudes, source_sites, spin_weights):
    groups = lax.axis_size("grp")
    sheets = lax.axis_size("lat")
    thick = gauge.shape[5]
    plane = gauge.shape[6]
    sides = amplitudes.shape[0]
    assert sides == groups and gauge.shape[4] == 1 and plane == 2 * LANES
    rows = 2 * thick * groups
    blocks = jnp.swapaxes(gauge.reshape(72, thick, 2, LANES), 1, 2).reshape(72, 2 * thick, LANES)
    smem = pl.BlockSpec(memory_space=pltpu.SMEM)
    out = pl.pallas_call(
        functools.partial(kernel, groups, sheets, thick),
        out_shape=jax.ShapeDtypeStruct((sides, 2, 4, 3, 2 * thick, LANES), jnp.float32),
        in_specs=[smem, smem, smem, pl.BlockSpec(memory_space=pl.ANY)],
        out_specs=pl.BlockSpec(memory_space=pl.ANY),
        scratch_shapes=[
            pltpu.VMEM((groups, 72, 2 * thick, LANES), jnp.float32),
            pltpu.VMEM((72, rows, LANES), jnp.float32),
            pltpu.VMEM((ITERS, 2, 2, 2, 3, rows, LANES), jnp.float32),
            pltpu.VMEM((ITERS, 2, 2, 2, 3, rows, LANES), jnp.float32),
            pltpu.VMEM((groups, 2, 4, 3, 2 * thick, LANES), jnp.float32),
            pltpu.VMEM((2, 4, 3, rows, LANES), jnp.float32),
            pltpu.SemaphoreType.DMA((3,)),
            pltpu.SemaphoreType.DMA((2, groups)),
            pltpu.SemaphoreType.DMA((2, groups)),
            pltpu.SemaphoreType.DMA((ITERS, 2)),
            pltpu.SemaphoreType.DMA((ITERS, 2)),
            pltpu.SemaphoreType.DMA((groups,)),
            pltpu.SemaphoreType.DMA((groups,)),
        ],
        compiler_params=pltpu.CompilerParams(
            collective_id=0, has_side_effects=True, vmem_limit_bytes=32 * 1024 * 1024
        ),
    )(amplitudes, source_sites, spin_weights, blocks)
    out = jnp.swapaxes(out.reshape(sides, 2, 4, 3, 2, thick, LANES), 4, 5)
    return out.reshape(sides, 2, 4, 3, 1, thick, plane)


def solution(mesh):
    placed = (
        P(None, None, None, None, "lat", "grp", None),
        P(None, None, None, "lat", None),
        P(None, "lat", None),
        P(),
    )
    return jax.shard_map(
        on_device,
        mesh=mesh,
        in_specs=placed,
        out_specs=P(None, None, None, None, "lat", "grp", None),
        check_vma=False,
    )
```

```python
import functools

import jax
import jax.numpy as jnp
from jax import lax
from jax.experimental import pallas as pl
from jax.experimental.pallas import tpu as pltpu
from jax.sharding import PartitionSpec as P

LXY = 16
LANES = 128
N_SMEAR = 4
ITERS = 4

smear_weight = 0.2
hop_kappa = 0.125
gamma_perm = ((3, 2, 1, 0), (3, 2, 1, 0), (2, 3, 0, 1), (2, 3, 0, 1))
gamma_phase = ((1, 1, 3, 3), (2, 0, 0, 2), (1, 3, 3, 1), (0, 0, 0, 0))


def phase_times(code, real, imag):
    if code == 0:
        return (real, imag)
    if code == 1:
        return (-imag, real)
    if code == 2:
        return (-real, -imag)
    return (imag, -real)


def project(hop_dir, sign, psi):
    re, im = psi
    rows_re, rows_im = [], []
    for spin in range(2):
        other = gamma_perm[hop_dir][spin]
        p_re, p_im = phase_times(gamma_phase[hop_dir][spin], re[other], im[other])
        if sign > 0:
            rows_re.append(re[spin] + p_re)
            rows_im.append(im[spin] + p_im)
        else:
            rows_re.append(re[spin] - p_re)
            rows_im.append(im[spin] - p_im)
    return jnp.stack(rows_re), jnp.stack(rows_im)


def add_rows(hop_dir, sign, total, half):
    t_re, t_im = list(total[0]), list(total[1])
    h_re, h_im = half
    for spin in range(2):
        t_re[spin] = t_re[spin] + h_re[spin]
        t_im[spin] = t_im[spin] + h_im[spin]
    for spin in (2, 3):
        other = gamma_perm[hop_dir][spin]
        p_re, p_im = phase_times(gamma_phase[hop_dir][spin], h_re[other], h_im[other])
        if sign > 0:
            t_re[spin] = t_re[spin] + p_re
            t_im[spin] = t_im[spin] + p_im
        else:
            t_re[spin] = t_re[spin] - p_re
            t_im[spin] = t_im[spin] - p_im
    return t_re, t_im


def times_link(links, half, adjoint):
    h_re, h_im = half
    out_re = out_im = None
    for b in range(3):
        if adjoint:
            u_re = links[0, b][None]
            u_im = -links[1, b][None]
        else:
            u_re = jnp.stack([links[0, a, b] for a in range(3)])[None]
            u_im = jnp.stack([links[1, a, b] for a in range(3)])[None]
        b_re = h_re[:, b][:, None]
        b_im = h_im[:, b][:, None]
        t_re = u_re * b_re - u_im * b_im
        t_im = u_re * b_im + u_im * b_re
        out_re = t_re if out_re is None else out_re + t_re
        out_im = t_im if out_im is None else out_im + t_im
    return out_re, out_im


def kernel(
    groups, sheets, thick, amp_hbm, site_hbm, weight_hbm, gauge_ref, out_ref,
    amp_ref, site_ref, weight_ref, recv, links, send_t, recv_t, stage, src,
    in_sem, own_sem, g_send, g_recv, t_send, t_recv, f_send, f_recv,
):
    nz = groups * thick
    rows = 2 * nz
    group = lax.axis_index("grp")
    sheet = lax.axis_index("lat")
    ahead = lax.rem(sheet + 1, sheets)
    behind = lax.rem(sheet + sheets - 1, sheets)
    parts = ((0, 54), (54, 18))

    own = [
        pltpu.make_async_copy(
            gauge_ref.at[pl.ds(lo, n)], recv.at[group, pl.ds(lo, n)], own_sem.at[i]
        )
        for i, (lo, n) in enumerate(parts)
    ]
    small = [
        pltpu.make_async_copy(amp_hbm, amp_ref, in_sem.at[0]),
        pltpu.make_async_copy(site_hbm, site_ref, in_sem.at[1]),
        pltpu.make_async_copy(weight_hbm, weight_ref, in_sem.at[2]),
    ]
    for copy in small + own:
        copy.start()

    barrier = pltpu.get_barrier_semaphore()
    for k in range(1, groups):
        pl.semaphore_signal(barrier, inc=1, device_id={"grp": lax.rem(group + k, groups)})
    pl.semaphore_signal(barrier, inc=1, device_id={"lat": ahead})
    pl.semaphore_signal(barrier, inc=1, device_id={"lat": behind})
    pl.semaphore_wait(barrier, groups + 1)

    def gauge_copy(part, k, slot):
        lo, n = parts[part]
        return pltpu.make_async_remote_copy(
            src_ref=gauge_ref.at[pl.ds(lo, n)],
            dst_ref=recv.at[slot, pl.ds(lo, n)],
            send_sem=g_send.at[part, k],
            recv_sem=g_recv.at[part, k],
            device_id={"grp": lax.rem(group + k, groups)},
        )

    for part in range(2):
        for k in range(1, groups):
            gauge_copy(part, k, group).start()

    row = lax.broadcasted_iota(jnp.int32, (rows, LANES), 0)
    lane = lax.broadcasted_iota(jnp.int32, (rows, LANES), 1)
    upper_half = row >= nz
    z = jnp.where(upper_half, row - nz, row)
    col = lane % LXY

    def shifted(field, hop_dir, offset):
        lanes_axis, rows_axis = field.ndim - 1, field.ndim - 2
        if hop_dir == 0:
            if offset > 0:
                return jnp.where(
                    col == LXY - 1,
                    pltpu.roll(field, LXY - 1, lanes_axis),
                    pltpu.roll(field, LANES - 1, lanes_axis),
                )
            return jnp.where(
                col == 0,
                pltpu.roll(field, LANES - LXY + 1, lanes_axis),
                pltpu.roll(field, 1, lanes_axis),
            )
        if hop_dir == 1:
            if offset > 0:
                rolled = pltpu.roll(field, LANES - LXY, lanes_axis)
                edge = lane >= LANES - LXY
            else:
                rolled = pltpu.roll(field, LXY, lanes_axis)
                edge = lane < LXY
            return jnp.where(edge, pltpu.roll(rolled, nz, rows_axis), rolled)
        if offset > 0:
            return jnp.where(
                z == nz - 1,
                pltpu.roll(field, nz - 1, rows_axis),
                pltpu.roll(field, rows - 1, rows_axis),
            )
        return jnp.where(
            z == 0,
            pltpu.roll(field, rows - nz + 1, rows_axis),
            pltpu.roll(field, 1, rows_axis),
        )

    def shifted_pair(pair, hop_dir, offset):
        return shifted(pair[0], hop_dir, offset), shifted(pair[1], hop_dir, offset)

    cells = z * (2 * LANES) + jnp.where(upper_half, LANES, 0) + lane
    points = site_ref.shape[2]

    def add_point(p, fields):
        hit = cells == site_ref[group, 0, p]
        return tuple(
            fields[i] + jnp.where(hit, amp_ref[group, i // 3, i % 3, 0, p], 0.0)
            for i in range(6)
        )

    for copy in small:
        copy.wait()
    zero = jnp.zeros((rows, LANES), jnp.float32)
    fields = lax.fori_loop(0, points, add_point, (zero,) * 6)
    colour = (jnp.stack(fields[:3])[None], jnp.stack(fields[3:])[None])

    def arrange(part):
        lo, n = parts[part]
        own[part].wait()
        for k in range(1, groups):
            gauge_copy(part, k, lax.rem(group + groups - k, groups)).wait_recv()
        for owner in range(groups):
            for half in range(2):
                to = half * nz + owner * thick
                links[pl.ds(lo, n), to : to + thick, :] = recv[
                    owner, pl.ds(lo, n), half * thick : (half + 1) * thick, :
                ]

    def link(hop_dir):
        class View:
            def __getitem__(self, index):
                base = hop_dir * 18 + index[0] * 9 + index[1] * 3
                if len(index) == 3:
                    return links[base + index[2]]
                return links[base : base + 3]

        return View()

    arrange(0)
    norm = 1.0 + 6.0 * smear_weight

    def smear(_, colour):
        total = None
        for hop_dir in range(3):
            fwd = times_link(link(hop_dir), shifted_pair(colour, hop_dir, 1), False)
            back = shifted_pair(times_link(link(hop_dir), colour, True), hop_dir, -1)
            add = (fwd[0] + back[0], fwd[1] + back[1])
            total = add if total is None else (total[0] + add[0], total[1] + add[1])
        return tuple(
            (1.0 / norm) * colour[i] + (smear_weight / norm) * total[i] for i in range(2)
        )

    colour = lax.fori_loop(0, N_SMEAR, smear, colour)
    c_re, c_im = colour[0][0], colour[1][0]
    for spin in range(4):
        w_re = weight_ref[group, 0, spin]
        w_im = weight_ref[group, 1, spin]
        src[0, spin] = w_re * c_re - w_im * c_im
        src[1, spin] = w_re * c_im + w_im * c_re

    arrange(1)
    sign_low = jnp.where(sheet == 0, -1.0, 1.0).astype(jnp.float32)
    sign_high = jnp.where(sheet == sheets - 1, -1.0, 1.0).astype(jnp.float32)

    def t_copy(step, way):
        return pltpu.make_async_remote_copy(
            src_ref=send_t.at[step, way],
            dst_ref=recv_t.at[step, way],
            send_sem=t_send.at[step, way],
            recv_sem=t_recv.at[step, way],
            device_id={"lat": behind if way == 0 else ahead},
        )

    def hop(step, psi):
        psi = (psi[0], psi[1])
        minus = project(3, -1, psi)
        send_t[step, 0, 0] = minus[0]
        send_t[step, 0, 1] = minus[1]
        t_copy(step, 0).start()
        plus = times_link(link(3), project(3, 1, psi), True)
        send_t[step, 1, 0] = plus[0]
        send_t[step, 1, 1] = plus[1]
        t_copy(step, 1).start()
        zeros = jnp.zeros((3, rows, LANES), jnp.float32)
        total = ([zeros] * 4, [zeros] * 4)
        for hop_dir in range(3):
            half = shifted_pair(project(hop_dir, -1, psi), hop_dir, 1)
            total = add_rows(hop_dir, -1, total, times_link(link(hop_dir), half, False))
            half = times_link(link(hop_dir), project(hop_dir, 1, psi), True)
            total = add_rows(hop_dir, 1, total, shifted_pair(half, hop_dir, -1))
        t_copy(step, 0).wait_recv()
        half = (sign_high * recv_t[step, 0, 0], sign_high * recv_t[step, 0, 1])
        total = add_rows(3, -1, total, times_link(link(3), half, False))
        t_copy(step, 1).wait_recv()
        half = (sign_low * recv_t[step, 1, 0], sign_low * recv_t[step, 1, 1])
        total = add_rows(3, 1, total, half)
        return tuple(src[i] + hop_kappa * jnp.stack(total[i]) for i in range(2))

    psi = lax.fori_loop(0, ITERS, hop, (src[0], src[1]))

    for owner in range(groups):
        for half in range(2):
            at = half * nz + owner * thick
            for i in range(2):
                stage[owner, i, :, :, half * thick : (half + 1) * thick, :] = psi[i][
                    :, :, at : at + thick, :
                ]

    def final_copy(k, slot, to):
        return pltpu.make_async_remote_copy(
            src_ref=stage.at[slot],
            dst_ref=out_ref.at[to],
            send_sem=f_send.at[k],
            recv_sem=f_recv.at[k],
            device_id={"grp": lax.rem(group + k, groups)},
        )

    for k in range(1, groups):
        final_copy(k, lax.rem(group + k, groups), group).start()
    mine = pltpu.make_async_copy(stage.at[group], out_ref.at[group], own_sem.at[2])
    mine.start()

    for part in range(2):
        for k in range(1, groups):
            gauge_copy(part, k, group).wait_send()
    for step in range(ITERS):
        for way in range(2):
            t_copy(step, way).wait_send()
    mine.wait()
    for k in range(1, groups):
        final_copy(k, lax.rem(group + k, groups), group).wait_send()
        final_copy(k, group, lax.rem(group + groups - k, groups)).wait_recv()


def on_device(gauge, amplitudes, source_sites, spin_weights):
    groups = lax.axis_size("grp")
    sheets = lax.axis_size("lat")
    thick = gauge.shape[5]
    plane = gauge.shape[6]
    sides = amplitudes.shape[0]
    assert sides == groups and gauge.shape[4] == 1 and plane == 2 * LANES
    rows = 2 * thick * groups
    blocks = jnp.swapaxes(gauge.reshape(72, thick, 2, LANES), 1, 2).reshape(72, 2 * thick, LANES)
    out = pl.pallas_call(
        functools.partial(kernel, groups, sheets, thick),
        out_shape=jax.ShapeDtypeStruct((sides, 2, 4, 3, 2 * thick, LANES), jnp.float32),
        in_specs=[pl.BlockSpec(memory_space=pl.ANY)] * 4,
        out_specs=pl.BlockSpec(memory_space=pl.ANY),
        scratch_shapes=[
            pltpu.SMEM(amplitudes.shape, jnp.float32),
            pltpu.SMEM(source_sites.shape, jnp.int32),
            pltpu.SMEM(spin_weights.shape, jnp.float32),
            pltpu.VMEM((groups, 72, 2 * thick, LANES), jnp.float32),
            pltpu.VMEM((72, rows, LANES), jnp.float32),
            pltpu.VMEM((ITERS, 2, 2, 2, 3, rows, LANES), jnp.float32),
            pltpu.VMEM((ITERS, 2, 2, 2, 3, rows, LANES), jnp.float32),
            pltpu.VMEM((groups, 2, 4, 3, 2 * thick, LANES), jnp.float32),
            pltpu.VMEM((2, 4, 3, rows, LANES), jnp.float32),
            pltpu.SemaphoreType.DMA((3,)),
            pltpu.SemaphoreType.DMA((3,)),
            pltpu.SemaphoreType.DMA((2, groups)),
            pltpu.SemaphoreType.DMA((2, groups)),
            pltpu.SemaphoreType.DMA((ITERS, 2)),
            pltpu.SemaphoreType.DMA((ITERS, 2)),
            pltpu.SemaphoreType.DMA((groups,)),
            pltpu.SemaphoreType.DMA((groups,)),
        ],
        compiler_params=pltpu.CompilerParams(
            collective_id=0, has_side_effects=True, vmem_limit_bytes=63 * 1024 * 1024
        ),
    )(amplitudes, source_sites, spin_weights, blocks)
    out = jnp.swapaxes(out.reshape(sides, 2, 4, 3, 2, thick, LANES), 4, 5)
    return out.reshape(sides, 2, 4, 3, 1, thick, plane)


def solution(mesh):
    placed = (
        P(None, None, None, None, "lat", "grp", None),
        P(None, None, None, "lat", None),
        P(None, "lat", None),
        P(),
    )
    return jax.shard_map(
        on_device,
        mesh=mesh,
        in_specs=placed,
        out_specs=P(None, None, None, None, "lat", "grp", None),
        check_vma=False,
    )
```

```python
import functools

import jax
import jax.numpy as jnp
from jax import lax
from jax.experimental import pallas as pl
from jax.experimental.pallas import tpu as pltpu
from jax.sharding import PartitionSpec as P

LXY = 16
LANES = 128
N_SMEAR = 4
ITERS = 4

smear_weight = 0.2
hop_kappa = 0.125
gamma_perm = ((3, 2, 1, 0), (3, 2, 1, 0), (2, 3, 0, 1), (2, 3, 0, 1))
gamma_phase = ((1, 1, 3, 3), (2, 0, 0, 2), (1, 3, 3, 1), (0, 0, 0, 0))


def phase_times(code, real, imag):
    if code == 0:
        return (real, imag)
    if code == 1:
        return (-imag, real)
    if code == 2:
        return (-real, -imag)
    return (imag, -real)


def project(hop_dir, sign, psi):
    re, im = psi
    rows_re, rows_im = [], []
    for spin in range(2):
        other = gamma_perm[hop_dir][spin]
        p_re, p_im = phase_times(gamma_phase[hop_dir][spin], re[other], im[other])
        if sign > 0:
            rows_re.append(re[spin] + p_re)
            rows_im.append(im[spin] + p_im)
        else:
            rows_re.append(re[spin] - p_re)
            rows_im.append(im[spin] - p_im)
    return jnp.stack(rows_re), jnp.stack(rows_im)


def add_rows(hop_dir, sign, total, half):
    t_re, t_im = list(total[0]), list(total[1])
    h_re, h_im = half
    for spin in range(2):
        t_re[spin] = t_re[spin] + h_re[spin]
        t_im[spin] = t_im[spin] + h_im[spin]
    for spin in (2, 3):
        other = gamma_perm[hop_dir][spin]
        p_re, p_im = phase_times(gamma_phase[hop_dir][spin], h_re[other], h_im[other])
        if sign > 0:
            t_re[spin] = t_re[spin] + p_re
            t_im[spin] = t_im[spin] + p_im
        else:
            t_re[spin] = t_re[spin] - p_re
            t_im[spin] = t_im[spin] - p_im
    return t_re, t_im


def times_link(links, half, adjoint):
    h_re, h_im = half
    out_re = out_im = None
    for b in range(3):
        if adjoint:
            u_re = links[0, b][None]
            u_im = -links[1, b][None]
        else:
            u_re = jnp.stack([links[0, a, b] for a in range(3)])[None]
            u_im = jnp.stack([links[1, a, b] for a in range(3)])[None]
        b_re = h_re[:, b][:, None]
        b_im = h_im[:, b][:, None]
        t_re = u_re * b_re - u_im * b_im
        t_im = u_re * b_im + u_im * b_re
        out_re = t_re if out_re is None else out_re + t_re
        out_im = t_im if out_im is None else out_im + t_im
    return out_re, out_im


def kernel(
    groups, sheets, thick, amp_hbm, site_hbm, weight_hbm, gauge_ref, out_ref,
    amp_ref, site_ref, weight_ref, recv, links, own_links, send_t, recv_t, send_z, recv_z,
    stage, src, in_sem, own_sem, g_send, g_recv, t_send, t_recv, z_send, z_recv,
):
    nz = groups * thick
    rows = 2 * nz
    sides = amp_ref.shape[0]
    block = 2 * thick
    group = lax.axis_index("grp")
    sheet = lax.axis_index("lat")
    ahead = lax.rem(sheet + 1, sheets)
    behind = lax.rem(sheet + sheets - 1, sheets)
    parts = ((0, 54), (54, 18))

    own = [
        pltpu.make_async_copy(
            gauge_ref.at[pl.ds(lo, n)], recv.at[group, pl.ds(lo, n)], own_sem.at[i]
        )
        for i, (lo, n) in enumerate(parts)
    ]
    small = [
        pltpu.make_async_copy(amp_hbm, amp_ref, in_sem.at[0]),
        pltpu.make_async_copy(site_hbm, site_ref, in_sem.at[1]),
        pltpu.make_async_copy(weight_hbm, weight_ref, in_sem.at[2]),
    ]
    for copy in small + own:
        copy.start()

    barrier = pltpu.get_barrier_semaphore()
    for k in range(1, groups):
        pl.semaphore_signal(barrier, inc=1, device_id={"grp": lax.rem(group + k, groups)})
    pl.semaphore_signal(barrier, inc=1, device_id={"lat": ahead})
    pl.semaphore_signal(barrier, inc=1, device_id={"lat": behind})
    pl.semaphore_wait(barrier, groups + 1)

    def gauge_copy(k, slot):
        lo, n = parts[0]
        return pltpu.make_async_remote_copy(
            src_ref=gauge_ref.at[pl.ds(lo, n)],
            dst_ref=recv.at[slot, pl.ds(lo, n)],
            send_sem=g_send.at[k],
            recv_sem=g_recv.at[k],
            device_id={"grp": lax.rem(group + k, groups)},
        )

    for k in range(1, groups):
        gauge_copy(k, group).start()

    row = lax.broadcasted_iota(jnp.int32, (rows, LANES), 0)
    lane = lax.broadcasted_iota(jnp.int32, (rows, LANES), 1)
    upper_half = row >= nz
    z = jnp.where(upper_half, row - nz, row)
    col = lane % LXY

    def shifted(field, hop_dir, offset):
        lanes_axis, rows_axis = field.ndim - 1, field.ndim - 2
        if hop_dir == 0:
            if offset > 0:
                return jnp.where(
                    col == LXY - 1,
                    pltpu.roll(field, LXY - 1, lanes_axis),
                    pltpu.roll(field, LANES - 1, lanes_axis),
                )
            return jnp.where(
                col == 0,
                pltpu.roll(field, LANES - LXY + 1, lanes_axis),
                pltpu.roll(field, 1, lanes_axis),
            )
        if hop_dir == 1:
            if offset > 0:
                rolled = pltpu.roll(field, LANES - LXY, lanes_axis)
                edge = lane >= LANES - LXY
            else:
                rolled = pltpu.roll(field, LXY, lanes_axis)
                edge = lane < LXY
            return jnp.where(edge, pltpu.roll(rolled, nz, rows_axis), rolled)
        if offset > 0:
            return jnp.where(
                z == nz - 1,
                pltpu.roll(field, nz - 1, rows_axis),
                pltpu.roll(field, rows - 1, rows_axis),
            )
        return jnp.where(
            z == 0,
            pltpu.roll(field, rows - nz + 1, rows_axis),
            pltpu.roll(field, 1, rows_axis),
        )

    def shifted_pair(pair, hop_dir, offset):
        return shifted(pair[0], hop_dir, offset), shifted(pair[1], hop_dir, offset)

    cells = z * (2 * LANES) + jnp.where(upper_half, LANES, 0) + lane
    points = site_ref.shape[2]

    def add_point(p, fields):
        hits = [cells == site_ref[side, 0, p] for side in range(sides)]
        return tuple(
            fields[i] + jnp.where(hits[i // 6], amp_ref[i // 6, i // 3 % 2, i % 3, 0, p], 0.0)
            for i in range(6 * sides)
        )

    for copy in small:
        copy.wait()
    zero = jnp.zeros((rows, LANES), jnp.float32)
    fields = lax.fori_loop(0, points, add_point, (zero,) * (6 * sides))
    colour = tuple(
        jnp.stack([jnp.stack(fields[6 * side + 3 * i :][:3]) for side in range(sides)])
        for i in range(2)
    )

    for copy in own:
        copy.wait()
    for side in range(sides):
        own_links[:, side * block : (side + 1) * block, :] = recv[group]
    for k in range(1, groups):
        gauge_copy(k, lax.rem(group + groups - k, groups)).wait_recv()
    lo, n = parts[0]
    for owner in range(groups):
        for half in range(2):
            to = half * nz + owner * thick
            links[:, to : to + thick, :] = recv[
                owner, lo : lo + n, half * thick : (half + 1) * thick, :
            ]

    def link(hop_dir, table):
        class View:
            def __getitem__(self, index):
                base = hop_dir * 18 + index[0] * 9 + index[1] * 3
                if len(index) == 3:
                    return table[base + index[2]]
                return table[base : base + 3]

        return View()

    norm = 1.0 + 6.0 * smear_weight

    def smear(_, colour):
        total = None
        for hop_dir in range(3):
            fwd = times_link(link(hop_dir, links), shifted_pair(colour, hop_dir, 1), False)
            back = shifted_pair(times_link(link(hop_dir, links), colour, True), hop_dir, -1)
            add = (fwd[0] + back[0], fwd[1] + back[1])
            total = add if total is None else (total[0] + add[0], total[1] + add[1])
        return tuple(
            (1.0 / norm) * colour[i] + (smear_weight / norm) * total[i] for i in range(2)
        )

    colour = lax.fori_loop(0, N_SMEAR, smear, colour)
    picked = []
    for i in range(2):
        pieces = []
        for side in range(sides):
            for half in range(2):
                piece = None
                for owner in range(groups):
                    at = half * nz + owner * thick
                    part = colour[i][side, :, at : at + thick, :]
                    piece = part if piece is None else jnp.where(group == owner, part, piece)
                pieces.append(piece)
        picked.append(jnp.concatenate(pieces, axis=1))
    c_re, c_im = picked
    hrows = sides * block
    hrow = lax.broadcasted_iota(jnp.int32, (hrows, LANES), 0)
    hlane = lax.broadcasted_iota(jnp.int32, (hrows, LANES), 1)
    hcol = hlane % LXY
    hz = hrow % thick
    low_half = hrow % block < thick
    for spin in range(4):
        w_re = jnp.full((hrows, LANES), weight_ref[0, 0, spin], jnp.float32)
        w_im = jnp.full((hrows, LANES), weight_ref[0, 1, spin], jnp.float32)
        for side in range(1, sides):
            w_re = jnp.where(hrow >= side * block, weight_ref[side, 0, spin], w_re)
            w_im = jnp.where(hrow >= side * block, weight_ref[side, 1, spin], w_im)
        src[0, spin] = w_re * c_re - w_im * c_im
        src[1, spin] = w_re * c_im + w_im * c_re

    def hshift(field, hop_dir, offset):
        lanes_axis, rows_axis = field.ndim - 1, field.ndim - 2
        if hop_dir == 0:
            fix = LXY - 1 if offset > 0 else LANES - LXY + 1
            move = LANES - 1 if offset > 0 else 1
            edge = hcol == (LXY - 1 if offset > 0 else 0)
            return jnp.where(
                edge, pltpu.roll(field, fix, lanes_axis), pltpu.roll(field, move, lanes_axis)
            )
        rolled = pltpu.roll(field, LANES - LXY if offset > 0 else LXY, lanes_axis)
        edge = hlane >= LANES - LXY if offset > 0 else hlane < LXY
        other = jnp.where(
            low_half,
            pltpu.roll(rolled, hrows - thick, rows_axis),
            pltpu.roll(rolled, thick, rows_axis),
        )
        return jnp.where(edge, other, rolled)

    def hshift_pair(pair, hop_dir, offset):
        return hshift(pair[0], hop_dir, offset), hshift(pair[1], hop_dir, offset)

    def z_copy(step, way):
        by = groups - 1 if way == 0 else 1
        return pltpu.make_async_remote_copy(
            src_ref=send_z.at[step],
            dst_ref=recv_z.at[step, way],
            send_sem=z_send.at[step, way],
            recv_sem=z_recv.at[step, way],
            device_id={"grp": lax.rem(group + by, groups)},
        )

    z_ways = 1 if groups == 2 else 2

    sign_low = jnp.where(sheet == 0, -1.0, 1.0).astype(jnp.float32)
    sign_high = jnp.where(sheet == sheets - 1, -1.0, 1.0).astype(jnp.float32)

    def t_copy(step, way):
        return pltpu.make_async_remote_copy(
            src_ref=send_t.at[step, way],
            dst_ref=recv_t.at[step, way],
            send_sem=t_send.at[step, way],
            recv_sem=t_recv.at[step, way],
            device_id={"lat": behind if way == 0 else ahead},
        )

    def hop(step, psi):
        psi = (psi[0], psi[1])
        minus = project(3, -1, psi)
        send_t[step, 0, 0] = minus[0]
        send_t[step, 0, 1] = minus[1]
        t_copy(step, 0).start()
        plus = times_link(link(3, own_links), project(3, 1, psi), True)
        send_t[step, 1, 0] = plus[0]
        send_t[step, 1, 1] = plus[1]
        t_copy(step, 1).start()
        z_ahead = project(2, -1, psi)
        z_back = times_link(link(2, own_links), project(2, 1, psi), True)
        for i in range(2):
            send_z[step, i] = jnp.where(hz == 0, z_ahead[i], z_back[i])
        for way in range(z_ways):
            z_copy(step, way).start()
        zeros = jnp.zeros((3, hrows, LANES), jnp.float32)
        total = ([zeros] * 4, [zeros] * 4)
        for hop_dir in range(2):
            half = hshift_pair(project(hop_dir, -1, psi), hop_dir, 1)
            total = add_rows(hop_dir, -1, total, times_link(link(hop_dir, own_links), half, False))
            half = times_link(link(hop_dir, own_links), project(hop_dir, 1, psi), True)
            total = add_rows(hop_dir, 1, total, hshift_pair(half, hop_dir, -1))
        for way in range(z_ways):
            z_copy(step, way).wait_recv()
        half = tuple(
            jnp.where(
                hz == thick - 1,
                pltpu.roll(recv_z[step, 0, i], thick - 1, 2),
                pltpu.roll(z_ahead[i], hrows - 1, 2),
            )
            for i in range(2)
        )
        total = add_rows(2, -1, total, times_link(link(2, own_links), half, False))
        half = tuple(
            jnp.where(
                hz == 0,
                pltpu.roll(recv_z[step, z_ways - 1, i], hrows - thick + 1, 2),
                pltpu.roll(z_back[i], 1, 2),
            )
            for i in range(2)
        )
        total = add_rows(2, 1, total, half)
        t_copy(step, 0).wait_recv()
        half = (sign_high * recv_t[step, 0, 0], sign_high * recv_t[step, 0, 1])
        total = add_rows(3, -1, total, times_link(link(3, own_links), half, False))
        t_copy(step, 1).wait_recv()
        half = (sign_low * recv_t[step, 1, 0], sign_low * recv_t[step, 1, 1])
        total = add_rows(3, 1, total, half)
        return tuple(src[i] + hop_kappa * jnp.stack(total[i]) for i in range(2))

    psi = lax.fori_loop(0, ITERS, hop, (src[0], src[1]))

    for side in range(sides):
        for i in range(2):
            stage[side, i] = psi[i][:, :, side * block : (side + 1) * block, :]
    done = pltpu.make_async_copy(stage, out_ref, own_sem.at[2])
    done.start()
    for k in range(1, groups):
        gauge_copy(k, group).wait_send()
    for step in range(ITERS):
        for way in range(2):
            t_copy(step, way).wait_send()
        for way in range(z_ways):
            z_copy(step, way).wait_send()
    done.wait()


def on_device(gauge, amplitudes, source_sites, spin_weights):
    groups = lax.axis_size("grp")
    sheets = lax.axis_size("lat")
    thick = gauge.shape[5]
    plane = gauge.shape[6]
    sides = amplitudes.shape[0]
    assert groups > 1 and gauge.shape[4] == 1 and plane == 2 * LANES
    rows = 2 * thick * groups
    hrows = 2 * thick * sides
    blocks = jnp.swapaxes(gauge.reshape(72, thick, 2, LANES), 1, 2).reshape(72, 2 * thick, LANES)
    out = pl.pallas_call(
        functools.partial(kernel, groups, sheets, thick),
        out_shape=jax.ShapeDtypeStruct((sides, 2, 4, 3, 2 * thick, LANES), jnp.float32),
        in_specs=[pl.BlockSpec(memory_space=pl.ANY)] * 4,
        out_specs=pl.BlockSpec(memory_space=pl.ANY),
        scratch_shapes=[
            pltpu.SMEM(amplitudes.shape, jnp.float32),
            pltpu.SMEM(source_sites.shape, jnp.int32),
            pltpu.SMEM(spin_weights.shape, jnp.float32),
            pltpu.VMEM((groups, 72, 2 * thick, LANES), jnp.float32),
            pltpu.VMEM((54, rows, LANES), jnp.float32),
            pltpu.VMEM((72, hrows, LANES), jnp.float32),
            pltpu.VMEM((ITERS, 2, 2, 2, 3, hrows, LANES), jnp.float32),
            pltpu.VMEM((ITERS, 2, 2, 2, 3, hrows, LANES), jnp.float32),
            pltpu.VMEM((ITERS, 2, 2, 3, hrows, LANES), jnp.float32),
            pltpu.VMEM((ITERS, 2, 2, 2, 3, hrows, LANES), jnp.float32),
            pltpu.VMEM((sides, 2, 4, 3, 2 * thick, LANES), jnp.float32),
            pltpu.VMEM((2, 4, 3, hrows, LANES), jnp.float32),
            pltpu.SemaphoreType.DMA((3,)),
            pltpu.SemaphoreType.DMA((3,)),
            pltpu.SemaphoreType.DMA((groups,)),
            pltpu.SemaphoreType.DMA((groups,)),
            pltpu.SemaphoreType.DMA((ITERS, 2)),
            pltpu.SemaphoreType.DMA((ITERS, 2)),
            pltpu.SemaphoreType.DMA((ITERS, 2)),
            pltpu.SemaphoreType.DMA((ITERS, 2)),
        ],
        compiler_params=pltpu.CompilerParams(
            collective_id=0, has_side_effects=True, vmem_limit_bytes=63 * 1024 * 1024
        ),
    )(amplitudes, source_sites, spin_weights, blocks)
    out = jnp.swapaxes(out.reshape(sides, 2, 4, 3, 2, thick, LANES), 4, 5)
    return out.reshape(sides, 2, 4, 3, 1, thick, plane)


def solution(mesh):
    placed = (
        P(None, None, None, None, "lat", "grp", None),
        P(None, None, None, "lat", None),
        P(None, "lat", None),
        P(),
    )
    return jax.shard_map(
        on_device,
        mesh=mesh,
        in_specs=placed,
        out_specs=P(None, None, None, None, "lat", "grp", None),
        check_vma=False,
    )
```

```python
import functools

import jax
import jax.numpy as jnp
from jax import lax
from jax.experimental import pallas as pl
from jax.experimental.pallas import tpu as pltpu
from jax.sharding import PartitionSpec as P

LXY = 16
LANES = 128
N_SMEAR = 4
ITERS = 4

smear_weight = 0.2
hop_kappa = 0.125
gamma_perm = ((3, 2, 1, 0), (3, 2, 1, 0), (2, 3, 0, 1), (2, 3, 0, 1))
gamma_phase = ((1, 1, 3, 3), (2, 0, 0, 2), (1, 3, 3, 1), (0, 0, 0, 0))


def phase_times(code, real, imag):
    if code == 0:
        return (real, imag)
    if code == 1:
        return (-imag, real)
    if code == 2:
        return (-real, -imag)
    return (imag, -real)


def project(hop_dir, sign, psi):
    re, im = psi
    rows_re, rows_im = [], []
    for spin in range(2):
        other = gamma_perm[hop_dir][spin]
        p_re, p_im = phase_times(gamma_phase[hop_dir][spin], re[other], im[other])
        if sign > 0:
            rows_re.append(re[spin] + p_re)
            rows_im.append(im[spin] + p_im)
        else:
            rows_re.append(re[spin] - p_re)
            rows_im.append(im[spin] - p_im)
    return jnp.stack(rows_re), jnp.stack(rows_im)


def add_rows(hop_dir, sign, total, half):
    t_re, t_im = list(total[0]), list(total[1])
    h_re, h_im = half
    for spin in range(2):
        t_re[spin] = t_re[spin] + h_re[spin]
        t_im[spin] = t_im[spin] + h_im[spin]
    for spin in (2, 3):
        other = gamma_perm[hop_dir][spin]
        p_re, p_im = phase_times(gamma_phase[hop_dir][spin], h_re[other], h_im[other])
        if sign > 0:
            t_re[spin] = t_re[spin] + p_re
            t_im[spin] = t_im[spin] + p_im
        else:
            t_re[spin] = t_re[spin] - p_re
            t_im[spin] = t_im[spin] - p_im
    return t_re, t_im


def times_link(links, half, adjoint):
    h_re, h_im = half
    out_re = out_im = None
    for b in range(3):
        if adjoint:
            u_re = links[0, b][None]
            u_im = -links[1, b][None]
        else:
            u_re = jnp.stack([links[0, a, b] for a in range(3)])[None]
            u_im = jnp.stack([links[1, a, b] for a in range(3)])[None]
        b_re = h_re[:, b][:, None]
        b_im = h_im[:, b][:, None]
        t_re = u_re * b_re - u_im * b_im
        t_im = u_re * b_im + u_im * b_re
        out_re = t_re if out_re is None else out_re + t_re
        out_im = t_im if out_im is None else out_im + t_im
    return out_re, out_im


def kernel(
    groups, sheets, thick, amp_hbm, site_hbm, weight_hbm, gauge_ref, out_ref,
    amp_ref, site_ref, weight_ref, recv, links, own_links, send_t, recv_t, send_z, recv_z,
    src, in_sem, own_sem, g_send, g_recv, t_send, t_recv, z_send, z_recv,
):
    nz = groups * thick
    rows = 2 * nz
    sides = amp_ref.shape[0]
    block = 2 * thick
    group = lax.axis_index("grp")
    sheet = lax.axis_index("lat")
    ahead = lax.rem(sheet + 1, sheets)
    behind = lax.rem(sheet + sheets - 1, sheets)
    parts = ((0, 54), (54, 18))

    own = [
        pltpu.make_async_copy(
            gauge_ref.at[pl.ds(lo, n)], recv.at[group, pl.ds(lo, n)], own_sem.at[i]
        )
        for i, (lo, n) in enumerate(parts)
    ]
    small = [
        pltpu.make_async_copy(amp_hbm, amp_ref, in_sem.at[0]),
        pltpu.make_async_copy(site_hbm, site_ref, in_sem.at[1]),
        pltpu.make_async_copy(weight_hbm, weight_ref, in_sem.at[2]),
    ]
    for copy in small + own:
        copy.start()

    barrier = pltpu.get_barrier_semaphore()
    for k in range(1, groups):
        pl.semaphore_signal(barrier, inc=1, device_id={"grp": lax.rem(group + k, groups)})
    pl.semaphore_signal(barrier, inc=1, device_id={"lat": ahead})
    pl.semaphore_signal(barrier, inc=1, device_id={"lat": behind})
    pl.semaphore_wait(barrier, groups + 1)

    def gauge_copy(k, slot):
        lo, n = parts[0]
        return pltpu.make_async_remote_copy(
            src_ref=gauge_ref.at[pl.ds(lo, n)],
            dst_ref=recv.at[slot, pl.ds(lo, n)],
            send_sem=g_send.at[k],
            recv_sem=g_recv.at[k],
            device_id={"grp": lax.rem(group + k, groups)},
        )

    for k in range(1, groups):
        gauge_copy(k, group).start()

    row = lax.broadcasted_iota(jnp.int32, (rows, LANES), 0)
    lane = lax.broadcasted_iota(jnp.int32, (rows, LANES), 1)
    upper_half = row >= nz
    z = jnp.where(upper_half, row - nz, row)
    col = lane % LXY

    def shifted(field, hop_dir, offset):
        lanes_axis, rows_axis = field.ndim - 1, field.ndim - 2
        if hop_dir == 0:
            if offset > 0:
                return jnp.where(
                    col == LXY - 1,
                    pltpu.roll(field, LXY - 1, lanes_axis),
                    pltpu.roll(field, LANES - 1, lanes_axis),
                )
            return jnp.where(
                col == 0,
                pltpu.roll(field, LANES - LXY + 1, lanes_axis),
                pltpu.roll(field, 1, lanes_axis),
            )
        if hop_dir == 1:
            if offset > 0:
                rolled = pltpu.roll(field, LANES - LXY, lanes_axis)
                edge = lane >= LANES - LXY
            else:
                rolled = pltpu.roll(field, LXY, lanes_axis)
                edge = lane < LXY
            return jnp.where(edge, pltpu.roll(rolled, nz, rows_axis), rolled)
        if offset > 0:
            return jnp.where(
                z == nz - 1,
                pltpu.roll(field, nz - 1, rows_axis),
                pltpu.roll(field, rows - 1, rows_axis),
            )
        return jnp.where(
            z == 0,
            pltpu.roll(field, rows - nz + 1, rows_axis),
            pltpu.roll(field, 1, rows_axis),
        )

    def shifted_pair(pair, hop_dir, offset):
        return shifted(pair[0], hop_dir, offset), shifted(pair[1], hop_dir, offset)

    cells = z * (2 * LANES) + jnp.where(upper_half, LANES, 0) + lane
    points = site_ref.shape[2]

    def add_point(p, fields):
        hits = [cells == site_ref[side, 0, p] for side in range(sides)]
        return tuple(
            fields[i] + jnp.where(hits[i // 6], amp_ref[i // 6, i // 3 % 2, i % 3, 0, p], 0.0)
            for i in range(6 * sides)
        )

    for copy in small:
        copy.wait()
    zero = jnp.zeros((rows, LANES), jnp.float32)
    fields = lax.fori_loop(0, points, add_point, (zero,) * (6 * sides))
    colour = tuple(
        jnp.stack([jnp.stack(fields[6 * side + 3 * i :][:3]) for side in range(sides)])
        for i in range(2)
    )

    for copy in own:
        copy.wait()
    for side in range(sides):
        own_links[:, side * block : (side + 1) * block, :] = recv[group]
    for k in range(1, groups):
        gauge_copy(k, lax.rem(group + groups - k, groups)).wait_recv()
    lo, n = parts[0]
    for owner in range(groups):
        for half in range(2):
            to = half * nz + owner * thick
            links[:, to : to + thick, :] = recv[
                owner, lo : lo + n, half * thick : (half + 1) * thick, :
            ]

    def link(hop_dir, table):
        class View:
            def __getitem__(self, index):
                base = hop_dir * 18 + index[0] * 9 + index[1] * 3
                if len(index) == 3:
                    return table[base + index[2]]
                return table[base : base + 3]

        return View()

    norm = 1.0 + 6.0 * smear_weight

    def smear(_, colour):
        total = None
        for hop_dir in range(3):
            fwd = times_link(link(hop_dir, links), shifted_pair(colour, hop_dir, 1), False)
            back = shifted_pair(times_link(link(hop_dir, links), colour, True), hop_dir, -1)
            add = (fwd[0] + back[0], fwd[1] + back[1])
            total = add if total is None else (total[0] + add[0], total[1] + add[1])
        return tuple(
            (1.0 / norm) * colour[i] + (smear_weight / norm) * total[i] for i in range(2)
        )

    colour = lax.fori_loop(0, N_SMEAR, smear, colour)
    picked = []
    for i in range(2):
        pieces = []
        for side in range(sides):
            for half in range(2):
                piece = None
                for owner in range(groups):
                    at = half * nz + owner * thick
                    part = colour[i][side, :, at : at + thick, :]
                    piece = part if piece is None else jnp.where(group == owner, part, piece)
                pieces.append(piece)
        picked.append(jnp.concatenate(pieces, axis=1))
    c_re, c_im = picked
    hrows = sides * block
    hrow = lax.broadcasted_iota(jnp.int32, (hrows, LANES), 0)
    hlane = lax.broadcasted_iota(jnp.int32, (hrows, LANES), 1)
    hcol = hlane % LXY
    hz = hrow % thick
    low_half = hrow % block < thick
    for spin in range(4):
        w_re = jnp.full((hrows, LANES), weight_ref[0, 0, spin], jnp.float32)
        w_im = jnp.full((hrows, LANES), weight_ref[0, 1, spin], jnp.float32)
        for side in range(1, sides):
            w_re = jnp.where(hrow >= side * block, weight_ref[side, 0, spin], w_re)
            w_im = jnp.where(hrow >= side * block, weight_ref[side, 1, spin], w_im)
        src[0, spin] = w_re * c_re - w_im * c_im
        src[1, spin] = w_re * c_im + w_im * c_re

    def hshift(field, hop_dir, offset):
        lanes_axis, rows_axis = field.ndim - 1, field.ndim - 2
        if hop_dir == 0:
            fix = LXY - 1 if offset > 0 else LANES - LXY + 1
            move = LANES - 1 if offset > 0 else 1
            edge = hcol == (LXY - 1 if offset > 0 else 0)
            return jnp.where(
                edge, pltpu.roll(field, fix, lanes_axis), pltpu.roll(field, move, lanes_axis)
            )
        rolled = pltpu.roll(field, LANES - LXY if offset > 0 else LXY, lanes_axis)
        edge = hlane >= LANES - LXY if offset > 0 else hlane < LXY
        other = jnp.where(
            low_half,
            pltpu.roll(rolled, hrows - thick, rows_axis),
            pltpu.roll(rolled, thick, rows_axis),
        )
        return jnp.where(edge, other, rolled)

    def hshift_pair(pair, hop_dir, offset):
        return hshift(pair[0], hop_dir, offset), hshift(pair[1], hop_dir, offset)

    def z_copy(step, way):
        by = groups - 1 if way == 0 else 1
        return pltpu.make_async_remote_copy(
            src_ref=send_z.at[step],
            dst_ref=recv_z.at[step, way],
            send_sem=z_send.at[step, way],
            recv_sem=z_recv.at[step, way],
            device_id={"grp": lax.rem(group + by, groups)},
        )

    z_ways = 1 if groups == 2 else 2

    sign_low = jnp.where(sheet == 0, -1.0, 1.0).astype(jnp.float32)
    sign_high = jnp.where(sheet == sheets - 1, -1.0, 1.0).astype(jnp.float32)

    def t_copy(step, way):
        return pltpu.make_async_remote_copy(
            src_ref=send_t.at[step, way],
            dst_ref=recv_t.at[step, way],
            send_sem=t_send.at[step, way],
            recv_sem=t_recv.at[step, way],
            device_id={"lat": behind if way == 0 else ahead},
        )

    def hop(step, psi):
        psi = (psi[0], psi[1])
        minus = project(3, -1, psi)
        send_t[step, 0, 0] = minus[0]
        send_t[step, 0, 1] = minus[1]
        t_copy(step, 0).start()
        plus = times_link(link(3, own_links), project(3, 1, psi), True)
        send_t[step, 1, 0] = plus[0]
        send_t[step, 1, 1] = plus[1]
        t_copy(step, 1).start()
        z_ahead = project(2, -1, psi)
        z_back = times_link(link(2, own_links), project(2, 1, psi), True)
        for i in range(2):
            send_z[step, i] = jnp.where(hz == 0, z_ahead[i], z_back[i])
        for way in range(z_ways):
            z_copy(step, way).start()
        zeros = jnp.zeros((3, hrows, LANES), jnp.float32)
        total = ([zeros] * 4, [zeros] * 4)
        for hop_dir in range(2):
            half = hshift_pair(project(hop_dir, -1, psi), hop_dir, 1)
            total = add_rows(hop_dir, -1, total, times_link(link(hop_dir, own_links), half, False))
            half = times_link(link(hop_dir, own_links), project(hop_dir, 1, psi), True)
            total = add_rows(hop_dir, 1, total, hshift_pair(half, hop_dir, -1))
        for way in range(z_ways):
            z_copy(step, way).wait_recv()
        half = tuple(
            jnp.where(
                hz == thick - 1,
                pltpu.roll(recv_z[step, 0, i], thick - 1, 2),
                pltpu.roll(z_ahead[i], hrows - 1, 2),
            )
            for i in range(2)
        )
        total = add_rows(2, -1, total, times_link(link(2, own_links), half, False))
        half = tuple(
            jnp.where(
                hz == 0,
                pltpu.roll(recv_z[step, z_ways - 1, i], hrows - thick + 1, 2),
                pltpu.roll(z_back[i], 1, 2),
            )
            for i in range(2)
        )
        total = add_rows(2, 1, total, half)
        t_copy(step, 0).wait_recv()
        half = (sign_high * recv_t[step, 0, 0], sign_high * recv_t[step, 0, 1])
        total = add_rows(3, -1, total, times_link(link(3, own_links), half, False))
        t_copy(step, 1).wait_recv()
        half = (sign_low * recv_t[step, 1, 0], sign_low * recv_t[step, 1, 1])
        total = add_rows(3, 1, total, half)
        return tuple(src[i] + hop_kappa * jnp.stack(total[i]) for i in range(2))

    psi = lax.fori_loop(0, ITERS, hop, (src[0], src[1]))

    for side in range(sides):
        for i in range(2):
            out_ref[side, i] = psi[i][:, :, side * block : (side + 1) * block, :]
    for k in range(1, groups):
        gauge_copy(k, group).wait_send()
    for step in range(ITERS):
        for way in range(2):
            t_copy(step, way).wait_send()
        for way in range(z_ways):
            z_copy(step, way).wait_send()


def on_device(gauge, amplitudes, source_sites, spin_weights):
    groups = lax.axis_size("grp")
    sheets = lax.axis_size("lat")
    thick = gauge.shape[5]
    plane = gauge.shape[6]
    sides = amplitudes.shape[0]
    assert groups > 1 and gauge.shape[4] == 1 and plane == 2 * LANES
    rows = 2 * thick * groups
    hrows = 2 * thick * sides
    blocks = jnp.swapaxes(gauge.reshape(72, thick, 2, LANES), 1, 2).reshape(72, 2 * thick, LANES)
    out = pl.pallas_call(
        functools.partial(kernel, groups, sheets, thick),
        out_shape=pltpu.VMEM((sides, 2, 4, 3, 2 * thick, LANES), jnp.float32),
        in_specs=[pl.BlockSpec(memory_space=pl.ANY)] * 4,
        out_specs=pl.BlockSpec(memory_space=pltpu.VMEM),
        scratch_shapes=[
            pltpu.SMEM(amplitudes.shape, jnp.float32),
            pltpu.SMEM(source_sites.shape, jnp.int32),
            pltpu.SMEM(spin_weights.shape, jnp.float32),
            pltpu.VMEM((groups, 72, 2 * thick, LANES), jnp.float32),
            pltpu.VMEM((54, rows, LANES), jnp.float32),
            pltpu.VMEM((72, hrows, LANES), jnp.float32),
            pltpu.VMEM((ITERS, 2, 2, 2, 3, hrows, LANES), jnp.float32),
            pltpu.VMEM((ITERS, 2, 2, 2, 3, hrows, LANES), jnp.float32),
            pltpu.VMEM((ITERS, 2, 2, 3, hrows, LANES), jnp.float32),
            pltpu.VMEM((ITERS, 2, 2, 2, 3, hrows, LANES), jnp.float32),
            pltpu.VMEM((2, 4, 3, hrows, LANES), jnp.float32),
            pltpu.SemaphoreType.DMA((3,)),
            pltpu.SemaphoreType.DMA((2,)),
            pltpu.SemaphoreType.DMA((groups,)),
            pltpu.SemaphoreType.DMA((groups,)),
            pltpu.SemaphoreType.DMA((ITERS, 2)),
            pltpu.SemaphoreType.DMA((ITERS, 2)),
            pltpu.SemaphoreType.DMA((ITERS, 2)),
            pltpu.SemaphoreType.DMA((ITERS, 2)),
        ],
        compiler_params=pltpu.CompilerParams(
            collective_id=0, has_side_effects=True, vmem_limit_bytes=63 * 1024 * 1024
        ),
    )(amplitudes, source_sites, spin_weights, blocks)
    out = jnp.swapaxes(out.reshape(sides, 2, 4, 3, 2, thick, LANES), 4, 5)
    return out.reshape(sides, 2, 4, 3, 1, thick, plane)


def solution(mesh):
    placed = (
        P(None, None, None, None, "lat", "grp", None),
        P(None, None, None, "lat", None),
        P(None, "lat", None),
        P(),
    )
    return jax.shard_map(
        on_device,
        mesh=mesh,
        in_specs=placed,
        out_specs=P(None, None, None, None, "lat", "grp", None),
        check_vma=False,
    )
```

```python
import functools

import jax
import jax.numpy as jnp
from jax import lax
from jax.experimental import pallas as pl
from jax.experimental.pallas import tpu as pltpu
from jax.sharding import PartitionSpec as P

LXY = 16
LANES = 128
N_SMEAR = 4
ITERS = 4

smear_weight = 0.2
hop_kappa = 0.125
gamma_perm = ((3, 2, 1, 0), (3, 2, 1, 0), (2, 3, 0, 1), (2, 3, 0, 1))
gamma_phase = ((1, 1, 3, 3), (2, 0, 0, 2), (1, 3, 3, 1), (0, 0, 0, 0))


def phase_times(code, real, imag):
    if code == 0:
        return (real, imag)
    if code == 1:
        return (-imag, real)
    if code == 2:
        return (-real, -imag)
    return (imag, -real)


def project(hop_dir, sign, psi):
    re, im = psi
    rows_re, rows_im = [], []
    for spin in range(2):
        other = gamma_perm[hop_dir][spin]
        p_re, p_im = phase_times(gamma_phase[hop_dir][spin], re[other], im[other])
        if sign > 0:
            rows_re.append(re[spin] + p_re)
            rows_im.append(im[spin] + p_im)
        else:
            rows_re.append(re[spin] - p_re)
            rows_im.append(im[spin] - p_im)
    return jnp.stack(rows_re), jnp.stack(rows_im)


def add_rows(hop_dir, sign, total, half):
    t_re, t_im = list(total[0]), list(total[1])
    h_re, h_im = half
    for spin in range(2):
        t_re[spin] = t_re[spin] + h_re[spin]
        t_im[spin] = t_im[spin] + h_im[spin]
    for spin in (2, 3):
        other = gamma_perm[hop_dir][spin]
        p_re, p_im = phase_times(gamma_phase[hop_dir][spin], h_re[other], h_im[other])
        if sign > 0:
            t_re[spin] = t_re[spin] + p_re
            t_im[spin] = t_im[spin] + p_im
        else:
            t_re[spin] = t_re[spin] - p_re
            t_im[spin] = t_im[spin] - p_im
    return t_re, t_im


def times_link(links, half, adjoint):
    h_re, h_im = half
    out_re = out_im = None
    for b in range(3):
        if adjoint:
            u_re = links[0, b][None]
            u_im = -links[1, b][None]
        else:
            u_re = jnp.stack([links[0, a, b] for a in range(3)])[None]
            u_im = jnp.stack([links[1, a, b] for a in range(3)])[None]
        b_re = h_re[:, b][:, None]
        b_im = h_im[:, b][:, None]
        t_re = u_re * b_re - u_im * b_im
        t_im = u_re * b_im + u_im * b_re
        out_re = t_re if out_re is None else out_re + t_re
        out_im = t_im if out_im is None else out_im + t_im
    return out_re, out_im


def kernel(
    groups, sheets, thick, amp_hbm, site_hbm, weight_hbm, gauge_ref, out_ref,
    amp_ref, site_ref, weight_ref, recv, links, own_links, send_t, recv_t, send_z, recv_z,
    src, in_sem, own_sem, g_send, g_recv, t_send, t_recv, z_send, z_recv,
):
    nz = groups * thick
    rows = 2 * nz
    sides = amp_ref.shape[0]
    block = 2 * thick
    group = lax.axis_index("grp")
    sheet = lax.axis_index("lat")
    ahead = lax.rem(sheet + 1, sheets)
    behind = lax.rem(sheet + sheets - 1, sheets)
    parts = ((0, 54), (54, 18))

    own = [
        pltpu.make_async_copy(
            gauge_ref.at[pl.ds(lo, n)], recv.at[group, pl.ds(lo, n)], own_sem.at[i]
        )
        for i, (lo, n) in enumerate(parts)
    ]
    small = [
        pltpu.make_async_copy(amp_hbm, amp_ref, in_sem.at[0]),
        pltpu.make_async_copy(site_hbm, site_ref, in_sem.at[1]),
        pltpu.make_async_copy(weight_hbm, weight_ref, in_sem.at[2]),
    ]
    for copy in small + own:
        copy.start()

    barrier = pltpu.get_barrier_semaphore()
    for k in range(1, groups):
        pl.semaphore_signal(barrier, inc=1, device_id={"grp": lax.rem(group + k, groups)})
    pl.semaphore_signal(barrier, inc=1, device_id={"lat": ahead})
    pl.semaphore_signal(barrier, inc=1, device_id={"lat": behind})
    pl.semaphore_wait(barrier, groups + 1)

    def gauge_copy(k, slot, hop_dir):
        lo, n = 18 * hop_dir, 18
        return pltpu.make_async_remote_copy(
            src_ref=gauge_ref.at[pl.ds(lo, n)],
            dst_ref=recv.at[slot, pl.ds(lo, n)],
            send_sem=g_send.at[hop_dir, k],
            recv_sem=g_recv.at[hop_dir, k],
            device_id={"grp": lax.rem(group + k, groups)},
        )

    for k in range(1, groups):
        for hop_dir in range(3):
            gauge_copy(k, group, hop_dir).start()

    row = lax.broadcasted_iota(jnp.int32, (rows, LANES), 0)
    lane = lax.broadcasted_iota(jnp.int32, (rows, LANES), 1)
    upper_half = row >= nz
    z = jnp.where(upper_half, row - nz, row)
    col = lane % LXY

    def shifted(field, hop_dir, offset):
        lanes_axis, rows_axis = field.ndim - 1, field.ndim - 2
        if hop_dir == 0:
            if offset > 0:
                return jnp.where(
                    col == LXY - 1,
                    pltpu.roll(field, LXY - 1, lanes_axis),
                    pltpu.roll(field, LANES - 1, lanes_axis),
                )
            return jnp.where(
                col == 0,
                pltpu.roll(field, LANES - LXY + 1, lanes_axis),
                pltpu.roll(field, 1, lanes_axis),
            )
        if hop_dir == 1:
            if offset > 0:
                rolled = pltpu.roll(field, LANES - LXY, lanes_axis)
                edge = lane >= LANES - LXY
            else:
                rolled = pltpu.roll(field, LXY, lanes_axis)
                edge = lane < LXY
            return jnp.where(edge, pltpu.roll(rolled, nz, rows_axis), rolled)
        if offset > 0:
            return jnp.where(
                z == nz - 1,
                pltpu.roll(field, nz - 1, rows_axis),
                pltpu.roll(field, rows - 1, rows_axis),
            )
        return jnp.where(
            z == 0,
            pltpu.roll(field, rows - nz + 1, rows_axis),
            pltpu.roll(field, 1, rows_axis),
        )

    def shifted_pair(pair, hop_dir, offset):
        return shifted(pair[0], hop_dir, offset), shifted(pair[1], hop_dir, offset)

    cells = z * (2 * LANES) + jnp.where(upper_half, LANES, 0) + lane
    points = site_ref.shape[2]

    def add_point(p, fields):
        hits = [cells == site_ref[side, 0, p] for side in range(sides)]
        return tuple(
            fields[i] + jnp.where(hits[i // 6], amp_ref[i // 6, i // 3 % 2, i % 3, 0, p], 0.0)
            for i in range(6 * sides)
        )

    for copy in small:
        copy.wait()
    zero = jnp.zeros((rows, LANES), jnp.float32)
    fields = lax.fori_loop(0, points, add_point, (zero,) * (6 * sides))
    colour = tuple(
        jnp.stack([jnp.stack(fields[6 * side + 3 * i :][:3]) for side in range(sides)])
        for i in range(2)
    )

    for copy in own:
        copy.wait()
    for side in range(sides):
        own_links[:, side * block : (side + 1) * block, :] = recv[group]
    for k in range(1, groups):
        for hop_dir in range(3):
            gauge_copy(k, lax.rem(group + groups - k, groups), hop_dir).wait_recv()
    lo, n = parts[0]
    for owner in range(groups):
        for half in range(2):
            to = half * nz + owner * thick
            links[:, to : to + thick, :] = recv[
                owner, lo : lo + n, half * thick : (half + 1) * thick, :
            ]

    def link(hop_dir, table):
        class View:
            def __getitem__(self, index):
                base = hop_dir * 18 + index[0] * 9 + index[1] * 3
                if len(index) == 3:
                    return table[base + index[2]]
                return table[base : base + 3]

        return View()

    norm = 1.0 + 6.0 * smear_weight

    def smear(_, colour):
        total = None
        for hop_dir in range(3):
            fwd = times_link(link(hop_dir, links), shifted_pair(colour, hop_dir, 1), False)
            back = shifted_pair(times_link(link(hop_dir, links), colour, True), hop_dir, -1)
            add = (fwd[0] + back[0], fwd[1] + back[1])
            total = add if total is None else (total[0] + add[0], total[1] + add[1])
        return tuple(
            (1.0 / norm) * colour[i] + (smear_weight / norm) * total[i] for i in range(2)
        )

    colour = lax.fori_loop(0, N_SMEAR, smear, colour)
    picked = []
    for i in range(2):
        pieces = []
        for side in range(sides):
            for half in range(2):
                piece = None
                for owner in range(groups):
                    at = half * nz + owner * thick
                    part = colour[i][side, :, at : at + thick, :]
                    piece = part if piece is None else jnp.where(group == owner, part, piece)
                pieces.append(piece)
        picked.append(jnp.concatenate(pieces, axis=1))
    c_re, c_im = picked
    hrows = sides * block
    hrow = lax.broadcasted_iota(jnp.int32, (hrows, LANES), 0)
    hlane = lax.broadcasted_iota(jnp.int32, (hrows, LANES), 1)
    hcol = hlane % LXY
    hz = hrow % thick
    low_half = hrow % block < thick
    for spin in range(4):
        w_re = jnp.full((hrows, LANES), weight_ref[0, 0, spin], jnp.float32)
        w_im = jnp.full((hrows, LANES), weight_ref[0, 1, spin], jnp.float32)
        for side in range(1, sides):
            w_re = jnp.where(hrow >= side * block, weight_ref[side, 0, spin], w_re)
            w_im = jnp.where(hrow >= side * block, weight_ref[side, 1, spin], w_im)
        src[0, spin] = w_re * c_re - w_im * c_im
        src[1, spin] = w_re * c_im + w_im * c_re

    def hshift(field, hop_dir, offset):
        lanes_axis, rows_axis = field.ndim - 1, field.ndim - 2
        if hop_dir == 0:
            fix = LXY - 1 if offset > 0 else LANES - LXY + 1
            move = LANES - 1 if offset > 0 else 1
            edge = hcol == (LXY - 1 if offset > 0 else 0)
            return jnp.where(
                edge, pltpu.roll(field, fix, lanes_axis), pltpu.roll(field, move, lanes_axis)
            )
        rolled = pltpu.roll(field, LANES - LXY if offset > 0 else LXY, lanes_axis)
        edge = hlane >= LANES - LXY if offset > 0 else hlane < LXY
        other = jnp.where(
            low_half,
            pltpu.roll(rolled, hrows - thick, rows_axis),
            pltpu.roll(rolled, thick, rows_axis),
        )
        return jnp.where(edge, other, rolled)

    def hshift_pair(pair, hop_dir, offset):
        return hshift(pair[0], hop_dir, offset), hshift(pair[1], hop_dir, offset)

    def z_copy(step, way):
        by = groups - 1 if way == 0 else 1
        return pltpu.make_async_remote_copy(
            src_ref=send_z.at[step],
            dst_ref=recv_z.at[step, way],
            send_sem=z_send.at[step, way],
            recv_sem=z_recv.at[step, way],
            device_id={"grp": lax.rem(group + by, groups)},
        )

    z_ways = 1 if groups == 2 else 2

    sign_low = jnp.where(sheet == 0, -1.0, 1.0).astype(jnp.float32)
    sign_high = jnp.where(sheet == sheets - 1, -1.0, 1.0).astype(jnp.float32)

    def t_copy(step, way, i):
        return pltpu.make_async_remote_copy(
            src_ref=send_t.at[step, way, i],
            dst_ref=recv_t.at[step, way, i],
            send_sem=t_send.at[step, way, i],
            recv_sem=t_recv.at[step, way, i],
            device_id={"lat": behind if way == 0 else ahead},
        )

    def hop(step, psi):
        psi = (psi[0], psi[1])
        minus = project(3, -1, psi)
        for i in range(2):
            send_t[step, 0, i] = minus[i]
            t_copy(step, 0, i).start()
        plus = times_link(link(3, own_links), project(3, 1, psi), True)
        for i in range(2):
            send_t[step, 1, i] = plus[i]
            t_copy(step, 1, i).start()
        z_ahead = project(2, -1, psi)
        z_back = times_link(link(2, own_links), project(2, 1, psi), True)
        for i in range(2):
            send_z[step, i] = jnp.where(hz == 0, z_ahead[i], z_back[i])
        for way in range(z_ways):
            z_copy(step, way).start()
        zeros = jnp.zeros((3, hrows, LANES), jnp.float32)
        total = ([zeros] * 4, [zeros] * 4)
        for hop_dir in range(2):
            half = hshift_pair(project(hop_dir, -1, psi), hop_dir, 1)
            total = add_rows(hop_dir, -1, total, times_link(link(hop_dir, own_links), half, False))
            half = times_link(link(hop_dir, own_links), project(hop_dir, 1, psi), True)
            total = add_rows(hop_dir, 1, total, hshift_pair(half, hop_dir, -1))
        for way in range(z_ways):
            z_copy(step, way).wait_recv()
        half = tuple(
            jnp.where(
                hz == thick - 1,
                pltpu.roll(recv_z[step, 0, i], thick - 1, 2),
                pltpu.roll(z_ahead[i], hrows - 1, 2),
            )
            for i in range(2)
        )
        total = add_rows(2, -1, total, times_link(link(2, own_links), half, False))
        half = tuple(
            jnp.where(
                hz == 0,
                pltpu.roll(recv_z[step, z_ways - 1, i], hrows - thick + 1, 2),
                pltpu.roll(z_back[i], 1, 2),
            )
            for i in range(2)
        )
        total = add_rows(2, 1, total, half)
        for i in range(2):
            t_copy(step, 0, i).wait_recv()
        half = (sign_high * recv_t[step, 0, 0], sign_high * recv_t[step, 0, 1])
        total = add_rows(3, -1, total, times_link(link(3, own_links), half, False))
        for i in range(2):
            t_copy(step, 1, i).wait_recv()
        half = (sign_low * recv_t[step, 1, 0], sign_low * recv_t[step, 1, 1])
        total = add_rows(3, 1, total, half)
        return tuple(src[i] + hop_kappa * jnp.stack(total[i]) for i in range(2))

    psi = lax.fori_loop(0, ITERS, hop, (src[0], src[1]))

    for side in range(sides):
        for i in range(2):
            out_ref[side, i] = psi[i][:, :, side * block : (side + 1) * block, :]
    for k in range(1, groups):
        for hop_dir in range(3):
            gauge_copy(k, group, hop_dir).wait_send()
    for step in range(ITERS):
        for way in range(2):
            for i in range(2):
                t_copy(step, way, i).wait_send()
        for way in range(z_ways):
            z_copy(step, way).wait_send()


def on_device(gauge, amplitudes, source_sites, spin_weights):
    groups = lax.axis_size("grp")
    sheets = lax.axis_size("lat")
    thick = gauge.shape[5]
    plane = gauge.shape[6]
    sides = amplitudes.shape[0]
    assert groups > 1 and gauge.shape[4] == 1 and plane == 2 * LANES
    rows = 2 * thick * groups
    hrows = 2 * thick * sides
    blocks = jnp.swapaxes(gauge.reshape(72, thick, 2, LANES), 1, 2).reshape(72, 2 * thick, LANES)
    out = pl.pallas_call(
        functools.partial(kernel, groups, sheets, thick),
        out_shape=pltpu.VMEM((sides, 2, 4, 3, 2 * thick, LANES), jnp.float32),
        in_specs=[pl.BlockSpec(memory_space=pl.ANY)] * 4,
        out_specs=pl.BlockSpec(memory_space=pltpu.VMEM),
        scratch_shapes=[
            pltpu.SMEM(amplitudes.shape, jnp.float32),
            pltpu.SMEM(source_sites.shape, jnp.int32),
            pltpu.SMEM(spin_weights.shape, jnp.float32),
            pltpu.VMEM((groups, 72, 2 * thick, LANES), jnp.float32),
            pltpu.VMEM((54, rows, LANES), jnp.float32),
            pltpu.VMEM((72, hrows, LANES), jnp.float32),
            pltpu.VMEM((ITERS, 2, 2, 2, 3, hrows, LANES), jnp.float32),
            pltpu.VMEM((ITERS, 2, 2, 2, 3, hrows, LANES), jnp.float32),
            pltpu.VMEM((ITERS, 2, 2, 3, hrows, LANES), jnp.float32),
            pltpu.VMEM((ITERS, 2, 2, 2, 3, hrows, LANES), jnp.float32),
            pltpu.VMEM((2, 4, 3, hrows, LANES), jnp.float32),
            pltpu.SemaphoreType.DMA((3,)),
            pltpu.SemaphoreType.DMA((2,)),
            pltpu.SemaphoreType.DMA((3, groups)),
            pltpu.SemaphoreType.DMA((3, groups)),
            pltpu.SemaphoreType.DMA((ITERS, 2, 2)),
            pltpu.SemaphoreType.DMA((ITERS, 2, 2)),
            pltpu.SemaphoreType.DMA((ITERS, 2)),
            pltpu.SemaphoreType.DMA((ITERS, 2)),
        ],
        compiler_params=pltpu.CompilerParams(
            collective_id=0, has_side_effects=True, vmem_limit_bytes=63 * 1024 * 1024
        ),
    )(amplitudes, source_sites, spin_weights, blocks)
    out = jnp.swapaxes(out.reshape(sides, 2, 4, 3, 2, thick, LANES), 4, 5)
    return out.reshape(sides, 2, 4, 3, 1, thick, plane)


def solution(mesh):
    placed = (
        P(None, None, None, None, "lat", "grp", None),
        P(None, None, None, "lat", None),
        P(None, "lat", None),
        P(),
    )
    return jax.shard_map(
        on_device,
        mesh=mesh,
        in_specs=placed,
        out_specs=P(None, None, None, None, "lat", "grp", None),
        check_vma=False,
    )
```

```python
import functools

import jax
import jax.numpy as jnp
from jax import lax
from jax.experimental import pallas as pl
from jax.experimental.pallas import tpu as pltpu
from jax.sharding import PartitionSpec as P

LXY = 16
LANES = 128
N_SMEAR = 4
ITERS = 4

smear_weight = 0.2
hop_kappa = 0.125
gamma_perm = ((3, 2, 1, 0), (3, 2, 1, 0), (2, 3, 0, 1), (2, 3, 0, 1))
gamma_phase = ((1, 1, 3, 3), (2, 0, 0, 2), (1, 3, 3, 1), (0, 0, 0, 0))


def phase_times(code, real, imag):
    if code == 0:
        return (real, imag)
    if code == 1:
        return (-imag, real)
    if code == 2:
        return (-real, -imag)
    return (imag, -real)


def project(hop_dir, sign, psi):
    re, im = psi
    rows_re, rows_im = [], []
    for spin in range(2):
        other = gamma_perm[hop_dir][spin]
        p_re, p_im = phase_times(gamma_phase[hop_dir][spin], re[other], im[other])
        if sign > 0:
            rows_re.append(re[spin] + p_re)
            rows_im.append(im[spin] + p_im)
        else:
            rows_re.append(re[spin] - p_re)
            rows_im.append(im[spin] - p_im)
    return jnp.stack(rows_re), jnp.stack(rows_im)


def add_rows(hop_dir, sign, total, half):
    t_re, t_im = list(total[0]), list(total[1])
    h_re, h_im = half
    for spin in range(2):
        t_re[spin] = t_re[spin] + h_re[spin]
        t_im[spin] = t_im[spin] + h_im[spin]
    for spin in (2, 3):
        other = gamma_perm[hop_dir][spin]
        p_re, p_im = phase_times(gamma_phase[hop_dir][spin], h_re[other], h_im[other])
        if sign > 0:
            t_re[spin] = t_re[spin] + p_re
            t_im[spin] = t_im[spin] + p_im
        else:
            t_re[spin] = t_re[spin] - p_re
            t_im[spin] = t_im[spin] - p_im
    return t_re, t_im


def times_link(links, half, adjoint):
    h_re, h_im = half
    out_re = out_im = None
    for b in range(3):
        if adjoint:
            u_re = links[0, b][None]
            u_im = -links[1, b][None]
        else:
            u_re = jnp.stack([links[0, a, b] for a in range(3)])[None]
            u_im = jnp.stack([links[1, a, b] for a in range(3)])[None]
        b_re = h_re[:, b][:, None]
        b_im = h_im[:, b][:, None]
        t_re = u_re * b_re - u_im * b_im
        t_im = u_re * b_im + u_im * b_re
        out_re = t_re if out_re is None else out_re + t_re
        out_im = t_im if out_im is None else out_im + t_im
    return out_re, out_im


def kernel(
    groups, sheets, thick, amp_hbm, site_hbm, weight_hbm, gauge_ref, out_ref,
    amp_ref, site_ref, weight_ref, recv, links, own_links, send_t, recv_t, send_z, recv_z,
    src, in_sem, own_sem, g_send, g_recv, t_send, t_recv, z_send, z_recv,
):
    nz = groups * thick
    rows = 2 * nz
    sides = amp_ref.shape[0]
    block = 2 * thick
    group = lax.axis_index("grp")
    sheet = lax.axis_index("lat")
    ahead = lax.rem(sheet + 1, sheets)
    behind = lax.rem(sheet + sheets - 1, sheets)
    parts = ((0, 54), (54, 18))

    own = [
        pltpu.make_async_copy(
            gauge_ref.at[pl.ds(lo, n)], recv.at[group, pl.ds(lo, n)], own_sem.at[i]
        )
        for i, (lo, n) in enumerate(parts)
    ]
    small = [
        pltpu.make_async_copy(amp_hbm, amp_ref, in_sem.at[0]),
        pltpu.make_async_copy(site_hbm, site_ref, in_sem.at[1]),
        pltpu.make_async_copy(weight_hbm, weight_ref, in_sem.at[2]),
    ]
    for copy in small + own:
        copy.start()

    barrier = pltpu.get_barrier_semaphore()
    for k in range(1, groups):
        pl.semaphore_signal(barrier, inc=1, device_id={"grp": lax.rem(group + k, groups)})
    pl.semaphore_signal(barrier, inc=1, device_id={"lat": ahead})
    pl.semaphore_signal(barrier, inc=1, device_id={"lat": behind})
    pl.semaphore_wait(barrier, groups + 1)

    def gauge_copy(k, slot):
        lo, n = parts[0]
        return pltpu.make_async_remote_copy(
            src_ref=gauge_ref.at[pl.ds(lo, n)],
            dst_ref=recv.at[slot, pl.ds(lo, n)],
            send_sem=g_send.at[k],
            recv_sem=g_recv.at[k],
            device_id={"grp": lax.rem(group + k, groups)},
        )

    for k in range(1, groups):
        gauge_copy(k, group).start()

    row = lax.broadcasted_iota(jnp.int32, (rows, LANES), 0)
    lane = lax.broadcasted_iota(jnp.int32, (rows, LANES), 1)
    upper_half = row >= nz
    z = jnp.where(upper_half, row - nz, row)
    col = lane % LXY

    def shifted(field, hop_dir, offset):
        lanes_axis, rows_axis = field.ndim - 1, field.ndim - 2
        if hop_dir == 0:
            if offset > 0:
                return jnp.where(
                    col == LXY - 1,
                    pltpu.roll(field, LXY - 1, lanes_axis),
                    pltpu.roll(field, LANES - 1, lanes_axis),
                )
            return jnp.where(
                col == 0,
                pltpu.roll(field, LANES - LXY + 1, lanes_axis),
                pltpu.roll(field, 1, lanes_axis),
            )
        if hop_dir == 1:
            if offset > 0:
                rolled = pltpu.roll(field, LANES - LXY, lanes_axis)
                edge = lane >= LANES - LXY
            else:
                rolled = pltpu.roll(field, LXY, lanes_axis)
                edge = lane < LXY
            return jnp.where(edge, pltpu.roll(rolled, nz, rows_axis), rolled)
        if offset > 0:
            return jnp.where(
                z == nz - 1,
                pltpu.roll(field, nz - 1, rows_axis),
                pltpu.roll(field, rows - 1, rows_axis),
            )
        return jnp.where(
            z == 0,
            pltpu.roll(field, rows - nz + 1, rows_axis),
            pltpu.roll(field, 1, rows_axis),
        )

    def shifted_pair(pair, hop_dir, offset):
        return shifted(pair[0], hop_dir, offset), shifted(pair[1], hop_dir, offset)

    cells = z * (2 * LANES) + jnp.where(upper_half, LANES, 0) + lane
    points = site_ref.shape[2]

    def add_point(p, fields):
        hits = [cells == site_ref[side, 0, p] for side in range(sides)]
        return tuple(
            fields[i] + jnp.where(hits[i // 6], amp_ref[i // 6, i // 3 % 2, i % 3, 0, p], 0.0)
            for i in range(6 * sides)
        )

    for copy in small:
        copy.wait()
    zero = jnp.zeros((rows, LANES), jnp.float32)
    fields = lax.fori_loop(0, points, add_point, (zero,) * (6 * sides))
    colour = tuple(
        jnp.stack([jnp.stack(fields[6 * side + 3 * i :][:3]) for side in range(sides)])
        for i in range(2)
    )

    for copy in own:
        copy.wait()
    for side in range(sides):
        own_links[:, side * block : (side + 1) * block, :] = recv[group]
    for k in range(1, groups):
        gauge_copy(k, lax.rem(group + groups - k, groups)).wait_recv()
    lo, n = parts[0]
    for owner in range(groups):
        for half in range(2):
            to = half * nz + owner * thick
            links[:, to : to + thick, :] = recv[
                owner, lo : lo + n, half * thick : (half + 1) * thick, :
            ]

    def link(hop_dir, table):
        class View:
            def __getitem__(self, index):
                base = hop_dir * 18 + index[0] * 9 + index[1] * 3
                if len(index) == 3:
                    return table[base + index[2]]
                return table[base : base + 3]

        return View()

    norm = 1.0 + 6.0 * smear_weight

    def smear(_, colour):
        total = None
        for hop_dir in range(3):
            fwd = times_link(link(hop_dir, links), shifted_pair(colour, hop_dir, 1), False)
            back = shifted_pair(times_link(link(hop_dir, links), colour, True), hop_dir, -1)
            add = (fwd[0] + back[0], fwd[1] + back[1])
            total = add if total is None else (total[0] + add[0], total[1] + add[1])
        return tuple(
            (1.0 / norm) * colour[i] + (smear_weight / norm) * total[i] for i in range(2)
        )

    colour = lax.fori_loop(0, N_SMEAR, smear, colour, unroll=True)
    picked = []
    for i in range(2):
        pieces = []
        for side in range(sides):
            for half in range(2):
                piece = None
                for owner in range(groups):
                    at = half * nz + owner * thick
                    part = colour[i][side, :, at : at + thick, :]
                    piece = part if piece is None else jnp.where(group == owner, part, piece)
                pieces.append(piece)
        picked.append(jnp.concatenate(pieces, axis=1))
    c_re, c_im = picked
    hrows = sides * block
    hrow = lax.broadcasted_iota(jnp.int32, (hrows, LANES), 0)
    hlane = lax.broadcasted_iota(jnp.int32, (hrows, LANES), 1)
    hcol = hlane % LXY
    hz = hrow % thick
    low_half = hrow % block < thick
    for spin in range(4):
        w_re = jnp.full((hrows, LANES), weight_ref[0, 0, spin], jnp.float32)
        w_im = jnp.full((hrows, LANES), weight_ref[0, 1, spin], jnp.float32)
        for side in range(1, sides):
            w_re = jnp.where(hrow >= side * block, weight_ref[side, 0, spin], w_re)
            w_im = jnp.where(hrow >= side * block, weight_ref[side, 1, spin], w_im)
        src[0, spin] = w_re * c_re - w_im * c_im
        src[1, spin] = w_re * c_im + w_im * c_re

    def hshift(field, hop_dir, offset):
        lanes_axis, rows_axis = field.ndim - 1, field.ndim - 2
        if hop_dir == 0:
            fix = LXY - 1 if offset > 0 else LANES - LXY + 1
            move = LANES - 1 if offset > 0 else 1
            edge = hcol == (LXY - 1 if offset > 0 else 0)
            return jnp.where(
                edge, pltpu.roll(field, fix, lanes_axis), pltpu.roll(field, move, lanes_axis)
            )
        rolled = pltpu.roll(field, LANES - LXY if offset > 0 else LXY, lanes_axis)
        edge = hlane >= LANES - LXY if offset > 0 else hlane < LXY
        other = jnp.where(
            low_half,
            pltpu.roll(rolled, hrows - thick, rows_axis),
            pltpu.roll(rolled, thick, rows_axis),
        )
        return jnp.where(edge, other, rolled)

    def hshift_pair(pair, hop_dir, offset):
        return hshift(pair[0], hop_dir, offset), hshift(pair[1], hop_dir, offset)

    def z_copy(step, way):
        by = groups - 1 if way == 0 else 1
        return pltpu.make_async_remote_copy(
            src_ref=send_z.at[step],
            dst_ref=recv_z.at[step, way],
            send_sem=z_send.at[step, way],
            recv_sem=z_recv.at[step, way],
            device_id={"grp": lax.rem(group + by, groups)},
        )

    z_ways = 1 if groups == 2 else 2

    sign_low = jnp.where(sheet == 0, -1.0, 1.0).astype(jnp.float32)
    sign_high = jnp.where(sheet == sheets - 1, -1.0, 1.0).astype(jnp.float32)

    def t_copy(step, way):
        return pltpu.make_async_remote_copy(
            src_ref=send_t.at[step, way],
            dst_ref=recv_t.at[step, way],
            send_sem=t_send.at[step, way],
            recv_sem=t_recv.at[step, way],
            device_id={"lat": behind if way == 0 else ahead},
        )

    def hop(step, psi):
        psi = (psi[0], psi[1])
        minus = project(3, -1, psi)
        send_t[step, 0, 0] = minus[0]
        send_t[step, 0, 1] = minus[1]
        t_copy(step, 0).start()
        plus = times_link(link(3, own_links), project(3, 1, psi), True)
        send_t[step, 1, 0] = plus[0]
        send_t[step, 1, 1] = plus[1]
        t_copy(step, 1).start()
        z_ahead = project(2, -1, psi)
        z_back = times_link(link(2, own_links), project(2, 1, psi), True)
        for i in range(2):
            send_z[step, i] = jnp.where(hz == 0, z_ahead[i], z_back[i])
        for way in range(z_ways):
            z_copy(step, way).start()
        zeros = jnp.zeros((3, hrows, LANES), jnp.float32)
        total = ([zeros] * 4, [zeros] * 4)
        for hop_dir in range(2):
            half = hshift_pair(project(hop_dir, -1, psi), hop_dir, 1)
            total = add_rows(hop_dir, -1, total, times_link(link(hop_dir, own_links), half, False))
            half = times_link(link(hop_dir, own_links), project(hop_dir, 1, psi), True)
            total = add_rows(hop_dir, 1, total, hshift_pair(half, hop_dir, -1))
        for way in range(z_ways):
            z_copy(step, way).wait_recv()
        half = tuple(
            jnp.where(
                hz == thick - 1,
                pltpu.roll(recv_z[step, 0, i], thick - 1, 2),
                pltpu.roll(z_ahead[i], hrows - 1, 2),
            )
            for i in range(2)
        )
        total = add_rows(2, -1, total, times_link(link(2, own_links), half, False))
        half = tuple(
            jnp.where(
                hz == 0,
                pltpu.roll(recv_z[step, z_ways - 1, i], hrows - thick + 1, 2),
                pltpu.roll(z_back[i], 1, 2),
            )
            for i in range(2)
        )
        total = add_rows(2, 1, total, half)
        t_copy(step, 0).wait_recv()
        half = (sign_high * recv_t[step, 0, 0], sign_high * recv_t[step, 0, 1])
        total = add_rows(3, -1, total, times_link(link(3, own_links), half, False))
        t_copy(step, 1).wait_recv()
        half = (sign_low * recv_t[step, 1, 0], sign_low * recv_t[step, 1, 1])
        total = add_rows(3, 1, total, half)
        return tuple(src[i] + hop_kappa * jnp.stack(total[i]) for i in range(2))

    psi = lax.fori_loop(0, ITERS, hop, (src[0], src[1]), unroll=True)

    for side in range(sides):
        for i in range(2):
            out_ref[side, i] = psi[i][:, :, side * block : (side + 1) * block, :]
    for k in range(1, groups):
        gauge_copy(k, group).wait_send()
    for step in range(ITERS):
        for way in range(2):
            t_copy(step, way).wait_send()
        for way in range(z_ways):
            z_copy(step, way).wait_send()


def on_device(gauge, amplitudes, source_sites, spin_weights):
    groups = lax.axis_size("grp")
    sheets = lax.axis_size("lat")
    thick = gauge.shape[5]
    plane = gauge.shape[6]
    sides = amplitudes.shape[0]
    assert groups > 1 and gauge.shape[4] == 1 and plane == 2 * LANES
    rows = 2 * thick * groups
    hrows = 2 * thick * sides
    blocks = jnp.swapaxes(gauge.reshape(72, thick, 2, LANES), 1, 2).reshape(72, 2 * thick, LANES)
    out = pl.pallas_call(
        functools.partial(kernel, groups, sheets, thick),
        out_shape=pltpu.VMEM((sides, 2, 4, 3, 2 * thick, LANES), jnp.float32),
        in_specs=[pl.BlockSpec(memory_space=pl.ANY)] * 4,
        out_specs=pl.BlockSpec(memory_space=pltpu.VMEM),
        scratch_shapes=[
            pltpu.SMEM(amplitudes.shape, jnp.float32),
            pltpu.SMEM(source_sites.shape, jnp.int32),
            pltpu.SMEM(spin_weights.shape, jnp.float32),
            pltpu.VMEM((groups, 72, 2 * thick, LANES), jnp.float32),
            pltpu.VMEM((54, rows, LANES), jnp.float32),
            pltpu.VMEM((72, hrows, LANES), jnp.float32),
            pltpu.VMEM((ITERS, 2, 2, 2, 3, hrows, LANES), jnp.float32),
            pltpu.VMEM((ITERS, 2, 2, 2, 3, hrows, LANES), jnp.float32),
            pltpu.VMEM((ITERS, 2, 2, 3, hrows, LANES), jnp.float32),
            pltpu.VMEM((ITERS, 2, 2, 2, 3, hrows, LANES), jnp.float32),
            pltpu.VMEM((2, 4, 3, hrows, LANES), jnp.float32),
            pltpu.SemaphoreType.DMA((3,)),
            pltpu.SemaphoreType.DMA((2,)),
            pltpu.SemaphoreType.DMA((groups,)),
            pltpu.SemaphoreType.DMA((groups,)),
            pltpu.SemaphoreType.DMA((ITERS, 2)),
            pltpu.SemaphoreType.DMA((ITERS, 2)),
            pltpu.SemaphoreType.DMA((ITERS, 2)),
            pltpu.SemaphoreType.DMA((ITERS, 2)),
        ],
        compiler_params=pltpu.CompilerParams(
            collective_id=0, has_side_effects=True, vmem_limit_bytes=63 * 1024 * 1024
        ),
    )(amplitudes, source_sites, spin_weights, blocks)
    out = jnp.swapaxes(out.reshape(sides, 2, 4, 3, 2, thick, LANES), 4, 5)
    return out.reshape(sides, 2, 4, 3, 1, thick, plane)


def solution(mesh):
    placed = (
        P(None, None, None, None, "lat", "grp", None),
        P(None, None, None, "lat", None),
        P(None, "lat", None),
        P(),
    )
    return jax.shard_map(
        on_device,
        mesh=mesh,
        in_specs=placed,
        out_specs=P(None, None, None, None, "lat", "grp", None),
        check_vma=False,
    )
```
